32 devices in a mesh: gx: 4 (over z), gy: 4 (over x, core), gz: 2 (over y).
Axes of the slice: x: 2, y: 2, z: 4, core: 2. Of those that a mesh axis runs over, the one named last changes fastest.
Arguments:
- right_side: float32 [16, 32, 256], P('gx', 'gy', 'gz'), may hold values from -8 to 8
- diagonal: float32 [16, 32, 256], P('gx', 'gy', 'gz'), may hold values from 0.2 to 2
- sign_bits: int32 [16, 32, 256], P('gx', 'gy', 'gz'), may hold values from 0 to 1
- freq_x: int32 [2048], replicated, may hold values from 0 to 15
- freq_y: int32 [2048], replicated, may hold values from 0 to 31
- freq_z: int32 [2048], replicated, may hold values from 0 to 255
Outputs:
- solution_field: float32 [16, 32, 256], P('gx', 'gy', 'gz')
- residual: float32 [16, 32, 256], P('gx', 'gy', 'gz')
The draws below stay inside these ranges and needn't reach their ends.
All inputs are finite; a program needn't handle non-finite values.
Results may differ from the reference program's by a relative error of at most 0.0009.
Values sent between devices are 32-bit elements; how exact they have to be, the bound alone decides.
A program may use at most 64 MiB of HBM per device.

```python
import math
import jax
import jax.numpy as jnp
from jax import lax

BASIS = 8
ITERS = 2
SKETCH = 2048
NX = 16
NY = 32
NZ = 256


def place_ends(entries, rng, least, largest):
    shape = entries.shape
    index_at = [jax.random.randint(jax.random.fold_in(rng, axis), (), 0, shape[axis]) for axis in range(len(shape))]
    entries = entries.at[tuple(index_at)].set(least)
    longest = shape.index(max(shape))
    index_at[longest] = (index_at[longest] + 1) % shape[longest]
    return entries.at[tuple(index_at)].set(largest)


def block_scale(own_key, shape, shards, least, largest):
    gain, own = 1.0, jax.random.fold_in(own_key, 6)
    for dim, shards_of in shards:
        heights = jnp.exp(jax.random.uniform(jax.random.fold_in(own, dim), (shards_of,), jnp.float32, least / len(shards), largest / len(shards)))
        gain = gain * jnp.repeat(heights, shape[dim] // shards_of).reshape([-1 if axis == dim else 1 for axis in range(len(shape))])
    return gain


def centred(own_key, extent, scale, reach, cuts=(), held_as=jnp.bfloat16):
    drawn = scale * jax.random.normal(own_key, extent, jnp.float32)
    if cuts:
        drawn = drawn * block_scale(own_key, extent, cuts, -0.22, 0.18)
    return jnp.clip(drawn, -reach, reach).astype(held_as)


def setup_inputs(seed: int = 0) -> dict:
    seeds = jax.random.split(jax.random.key(seed), 7)
    return {
        "right_side": centred(seeds[0], (NX, NY, NZ), 1.0, 8.0, ((0, 4), (1, 4), (2, 2)), jnp.float32),
        "diagonal": jnp.clip(jnp.exp(math.log(2.0) - 2.3025851 * jax.random.uniform(seeds[1], (NX, NY, NZ), jnp.float32) ** block_scale(seeds[1], (NX, NY, NZ), ((0, 4), (1, 4), (2, 2)), -0.2, 0.2)), 0.2, 2.0),
        "sign_bits": place_ends(jax.random.randint(seeds[2], (NX, NY, NZ), 0, 2), jax.random.fold_in(seeds[2], 1), 0, 1).astype(jnp.int32),
        "freq_x": place_ends(jax.random.randint(seeds[3], (SKETCH,), 0, NX), jax.random.fold_in(seeds[3], 1), 0, NX - 1).astype(jnp.int32),
        "freq_y": place_ends(jax.random.randint(seeds[4], (SKETCH,), 0, NY), jax.random.fold_in(seeds[4], 1), 0, NY - 1).astype(jnp.int32),
        "freq_z": place_ends(jax.random.randint(seeds[5], (SKETCH,), 0, NZ), jax.random.fold_in(seeds[5], 1), 0, NZ - 1).astype(jnp.int32),
    }


center_value = 7.0
half_range = 7.0
tiny_value = 1e-06
highest = lax.Precision.HIGHEST

def stencil(padded, diagonal):
    beside = padded[2:, 1:-1, 1:-1] + padded[:-2, 1:-1, 1:-1]
    beside = beside + padded[1:-1, 2:, 1:-1] + padded[1:-1, :-2, 1:-1]
    beside = beside + padded[1:-1, 1:-1, 2:] + padded[1:-1, 1:-1, :-2]
    return (6.0 + diagonal) * padded[1:-1, 1:-1, 1:-1] - beside

def cosine_table(freqs, count, length):
    indices = jnp.arange(count, dtype=jnp.int32)
    phases = (2 * indices[:, None] + 1) * freqs[None, :].astype(jnp.int32) % (4 * length)
    return (jnp.sqrt(2.0 / length) * jnp.cos(jnp.pi * phases / (2.0 * length))).astype(jnp.float32)

def least_squares(matrix):
    count = matrix.shape[0] - 1
    target = matrix[count]
    orthonormal = []
    upper = {}
    for column_at in range(count):
        column = matrix[column_at]
        for repeat in range(2):
            for earlier in range(column_at):
                amount = jnp.dot(orthonormal[earlier], column, precision=highest)
                column = column - amount * orthonormal[earlier]
                upper[earlier, column_at] = upper.get((earlier, column_at), 0.0) + amount
        length = jnp.sqrt(jnp.dot(column, column, precision=highest) + tiny_value)
        orthonormal.append(column / length)
        upper[column_at, column_at] = length
    projected = [jnp.dot(basis_row, target, precision=highest) for basis_row in orthonormal]
    solved = [None] * count
    for row_at in range(count - 1, -1, -1):
        value = projected[row_at]
        for later in range(row_at + 1, count):
            value = value - upper[row_at, later] * solved[later]
        solved[row_at] = value / upper[row_at, row_at]
    return jnp.stack(solved)

def chebyshev(residual, diagonal):
    vectors = [residual]
    images = []
    for position in range(BASIS):
        image = stencil(jnp.pad(vectors[position], 1), diagonal)
        images.append(image)
        if position + 1 < BASIS:
            turned = (image - center_value * vectors[position]) / half_range
            vectors.append(turned if position == 0 else 2.0 * turned - vectors[position - 1])
    return (vectors, images)

def sketch(columns, signs, table_x, table_y, table_z):
    flipped = jnp.stack(columns, axis=2) * signs[:, :, None, :]

    def per_slab(carry, inputs):
        slab_rows, row_x = inputs
        inner_sums = jnp.einsum('yjz,zs->yjs', slab_rows, table_z, precision=highest)
        weights = row_x[None, :] * table_y
        return (carry + jnp.einsum('yjs,ys->js', inner_sums, weights, precision=highest), None)
    start = jnp.zeros((len(columns), table_z.shape[1]), jnp.float32)
    summed, _ = lax.scan(per_slab, start, (flipped, table_x))
    return summed

def reference(right_side, diagonal, sign_bits, freq_x, freq_y, freq_z):
    size_x, size_y, size_z = right_side.shape
    table_x = cosine_table(freq_x, size_x, size_x)
    table_y = cosine_table(freq_y, size_y, size_y)
    table_z = cosine_table(freq_z, size_z, size_z)
    signs = 1.0 - 2.0 * sign_bits.astype(jnp.float32)
    solution = jnp.zeros_like(right_side)
    residual = right_side
    for restart in range(ITERS):
        vectors, images = chebyshev(residual, diagonal)
        matrix = sketch(images + [residual], signs, table_x, table_y, table_z)
        weights_solved = least_squares(matrix)
        for position in range(BASIS):
            solution = solution + weights_solved[position] * vectors[position]
            residual = residual - weights_solved[position] * images[position]
    return (solution, residual)
```

```python
import functools
import math

import jax
import jax.numpy as jnp
from jax import lax
from jax.experimental import pallas as pl
from jax.experimental.pallas import tpu as pltpu
from jax.sharding import PartitionSpec as P

BASIS = 8
ITERS = 2


center_value = 7.0
half_range = 7.0
tiny_value = 1e-06
highest = lax.Precision.HIGHEST


def extended(shard, sides, width):
    for axis, dim in sides:
        size, length = (lax.axis_size(axis), shard.shape[dim])
        up = [(i, (i + 1) % size) for i in range(size - 1)]
        down = [(j, i) for i, j in up]
        last = lax.slice_in_dim(shard, length - width, length, axis=dim)
        first = lax.slice_in_dim(shard, 0, width, axis=dim)
        before = lax.ppermute(last, axis, up)
        after = lax.ppermute(first, axis, down)
        shard = jnp.concatenate([before, shard, after], axis=dim)
    return shard


def stencil(padded, diagonal):
    beside = padded[2:, 1:-1, 1:-1] + padded[:-2, 1:-1, 1:-1]
    beside = beside + padded[1:-1, 2:, 1:-1] + padded[1:-1, :-2, 1:-1]
    beside = beside + padded[1:-1, 1:-1, 2:] + padded[1:-1, 1:-1, :-2]
    return (6.0 + diagonal) * padded[1:-1, 1:-1, 1:-1] - beside


def cosine_table(freqs, offset, count, length):
    indices = offset + jnp.arange(count, dtype=jnp.int32)
    phases = (2 * indices[:, None] + 1) * freqs[None, :] % (4 * length)
    return (jnp.sqrt(2.0 / length) * jnp.cos(jnp.pi * phases / (2.0 * length))).astype(jnp.float32)


def least_squares(matrix):
    count = matrix.shape[0] - 1
    target = matrix[count]
    orthonormal = []
    upper = {}
    for column_at in range(count):
        column = matrix[column_at]
        for repeat in range(2):
            for earlier in range(column_at):
                amount = jnp.dot(orthonormal[earlier], column, precision=highest)
                column = column - amount * orthonormal[earlier]
                upper[earlier, column_at] = upper.get((earlier, column_at), 0.0) + amount
        length = jnp.sqrt(jnp.dot(column, column, precision=highest) + tiny_value)
        orthonormal.append(column / length)
        upper[column_at, column_at] = length
    projected = [jnp.dot(basis_row, target, precision=highest) for basis_row in orthonormal]
    solved = [None] * count
    for row_at in range(count - 1, -1, -1):
        value = projected[row_at]
        for later in range(row_at + 1, count):
            value = value - upper[row_at, later] * solved[later]
        solved[row_at] = value / upper[row_at, row_at]
    return jnp.stack(solved)


def basis_plain(residual, diagonal):
    vectors = [residual]
    images = []
    for position in range(BASIS):
        padded = extended(vectors[position], (("gx", 0), ("gy", 1), ("gz", 2)), 1)
        image = stencil(padded, diagonal)
        images.append(image)
        if position + 1 < BASIS:
            turned = (image - center_value * vectors[position]) / half_range
            vectors.append(turned if position == 0 else 2.0 * turned - vectors[position - 1])
    return (vectors, images)


def local_sketch(columns, signs, table_x, table_y, table_z):
    flipped = jnp.stack(columns, axis=2) * signs[:, :, None, :]
    size_x, size_y, count, depth = flipped.shape
    rows_flat = flipped.reshape(-1, depth)
    weights = table_x[:, None, :] * table_y[None, :, :]
    sampled = table_z.shape[1]
    block = min(512, sampled)
    pieces = []
    for begin in range(0, sampled, block):
        inner_sums = jnp.dot(
            rows_flat,
            table_z[:, begin : begin + block],
            precision=highest,
            preferred_element_type=jnp.float32,
        )
        inner_sums = inner_sums.reshape(size_x, size_y, count, block)
        pieces.append(
            jnp.einsum(
                "xyjs,xys->js", inner_sums, weights[:, :, begin : begin + block], precision=highest
            )
        )
    return jnp.concatenate(pieces, axis=1)


def shards(right_side, diagonal, sign_bits, freq_x, freq_y, freq_z):
    size_x, size_y, size_z = right_side.shape
    table_x = cosine_table(
        freq_x, lax.axis_index("gx") * size_x, size_x, size_x * lax.axis_size("gx")
    )
    table_y = cosine_table(
        freq_y, lax.axis_index("gy") * size_y, size_y, size_y * lax.axis_size("gy")
    )
    table_z = cosine_table(
        freq_z, lax.axis_index("gz") * size_z, size_z, size_z * lax.axis_size("gz")
    )
    signs = 1.0 - 2.0 * sign_bits.astype(jnp.float32)
    solution = jnp.zeros_like(right_side)
    residual = right_side
    for restart in range(ITERS):
        vectors, images = basis_plain(residual, diagonal)
        partial_value = local_sketch(images + [residual], signs, table_x, table_y, table_z)
        shares = lax.psum_scatter(partial_value, "gx", scatter_dimension=1, tiled=True)
        shares = lax.psum(shares, ("gy", "gz"))
        matrix = lax.all_gather(shares, "gx", axis=1, tiled=True)
        weights_solved = least_squares(matrix)
        for position in range(BASIS):
            solution = solution + weights_solved[position] * vectors[position]
            residual = residual - weights_solved[position] * images[position]
    return (solution, residual)


MESH = pl.DeviceIdType.MESH
LANES = 128
SINE = [(-1.0) ** k / math.factorial(2 * k + 1) for k in range(7)]


def cosines(freqs, count, length):
    cells = lax.broadcasted_iota(jnp.int32, (count, freqs.shape[1]), 0)
    phases = lax.rem((2 * cells + 1) * freqs, 4 * length)
    folded = length - jnp.minimum(phases, 4 * length - phases)
    angle = folded.astype(jnp.float32) * (math.pi / (2.0 * length))
    square = angle * angle
    value = jnp.full_like(angle, SINE[-1])
    for term in SINE[-2::-1]:
        value = value * square + term
    return value * angle * math.sqrt(2.0 / length)


def total_of(value):
    return jnp.sum(jnp.sum(value, axis=0, keepdims=True), axis=1, keepdims=True)


def solve_rows(rows, target):
    count = len(rows)
    basis, among, short, upper, inverse = [], [], [], {}, []
    for at_column in range(count):
        column = rows[at_column]
        for repeat in range(2):
            left = [total_of(q * column) for q in basis]
            amounts = []
            for e in range(at_column):
                amount = left[e]
                amounts.append(amount)
                left[e] = amount * short[e]
                for f in range(at_column):
                    if f != e:
                        left[f] = left[f] - amount * among[max(e, f)][min(e, f)]
            for e in range(at_column):
                column = column - amounts[e] * basis[e]
                upper[e, at_column] = upper.get((e, at_column), 0.0) + amounts[e]
        length = jnp.sqrt(total_of(column * column) + tiny_value)
        scale = 1.0 / length
        basis.append(column * scale)
        among.append([value * scale for value in left] if at_column else [])
        short.append(tiny_value * scale * scale)
        inverse.append(scale)
    projected = [total_of(q * target) for q in basis]
    solved = [None] * count
    for row in range(count - 1, -1, -1):
        value = projected[row]
        for later in range(row + 1, count):
            value = value - upper[row, later] * solved[later]
        solved[row] = value * inverse[row]
    return solved


class Gather:
    def __init__(self, sizes, block, send_sem, recv_sem):
        self.sizes, self.block = sizes, block
        self.send_sem, self.recv_sem = send_sem, recv_sem
        self.count = 0
        self.at = {axis: lax.axis_index(axis) for axis in sizes}
        self.started = []

    def regions(self, ref, state, at):
        bx, by, bz = self.block
        gx, gy, gz = at["gx"], at["gy"], at["gz"]
        xs = slice(None) if state["x"] == "all" else pl.ds(gx * bx, bx)
        zs = slice(None) if state["z"] == "all" else pl.ds(pl.multiple_of(gz * bz, bz), bz)
        if state["y"] == "own":
            ys = [gy]
        else:
            ys = [lax.rem(gy, 2) + 2 * k for k in range(self.sizes["gy"] // 2)]
        return [ref.at[xs, pl.ds(pl.multiple_of(y * by, by), by), zs] for y in ys]

    def start(self, ref, state, phase):
        axis = {"X": "gx", "Z": "gz", "H": "gy", "C": "gy"}[phase]
        size, here = self.sizes[axis], self.at[axis]
        if phase == "C":
            hops = [(here + 1 - 2 * lax.rem(here, 2), here + 1 - 2 * lax.rem(here, 2))]
        else:
            stride = 2 if phase == "H" else 1
            hops = [
                (lax.rem(here + k, size), lax.rem(here + size - k, size))
                for k in range(stride, size, stride)
            ]
        arriving = []
        for target, origin in hops:
            mine = self.regions(ref, state, self.at)
            theirs = self.regions(ref, state, {**self.at, axis: origin})
            for source, landing in zip(mine, theirs):
                n = self.count
                self.count += 1
                sems = dict(send_sem=self.send_sem.at[n], recv_sem=self.recv_sem.at[n])
                go = dict(device_id={axis: target}, device_id_type=MESH)
                copy = pltpu.make_async_remote_copy(src_ref=source, dst_ref=source, **sems, **go)
                copy.start()
                self.started.append(copy)
                arriving.append(
                    pltpu.make_async_remote_copy(src_ref=landing, dst_ref=landing, **sems, **go)
                )
        if phase == "X":
            state["x"] = "all"
        elif phase == "Z":
            state["z"] = "all"
        elif phase == "H":
            state["y"] = "half"
        else:
            state["y"] = "all"
        return arriving


def copies_needed(sizes):
    half = sizes["gy"] // 2
    return 3 * (sizes["gx"] - 1 + (sizes["gz"] - 1) * half + half - 1 + half) + 8


def whole_kernel(
    sizes, share, right_ref, diagonal_ref, bits_ref, fx_ref, fy_ref, fz_ref, sol_ref, res_ref,
    field, diag, sign, vectors, images, flipped, table, weights, rows, sums, send_sem, recv_sem,
    small_send, small_recv,
):
    bx, by, bz = right_ref.shape
    nx, ny, nz = field.shape
    wide = table.shape[1]
    at = {axis: lax.axis_index(axis) for axis in sizes}

    barrier = pltpu.get_barrier_semaphore()
    peers = 0
    for axis, size in sizes.items():
        for k in range(1, size):
            target = lax.rem(at[axis] + k, size)
            pl.semaphore_signal(barrier, inc=1, device_id={axis: target}, device_id_type=MESH)
            peers += 1
    x0 = at["gx"] * bx
    y0 = pl.multiple_of(at["gy"] * by, by)
    z0 = pl.multiple_of(at["gz"] * bz, bz)
    own = (pl.ds(x0, bx), pl.ds(y0, by), pl.ds(z0, bz))
    field[own] = right_ref[...]
    diag[own] = diagonal_ref[...]
    sign[own] = 1.0 - 2.0 * bits_ref[...].astype(jnp.float32)
    pl.semaphore_wait(barrier, peers)

    gather = Gather(sizes, (bx, by, bz), send_sem, recv_sem)
    orders = [(field, "XZHC"), (diag, "XHZC"), (sign, "XZHC")]
    states = [{"x": "own", "y": "own", "z": "own"} for _ in orders]

    def begin(step):
        arriving = []
        for (ref, order), state in zip(orders, states):
            arriving += gather.start(ref, state, order[step])
        return arriving

    arriving = begin(0)
    me = (at["gx"] * sizes["gy"] + at["gy"]) * sizes["gz"] + at["gz"]
    lane = lax.broadcasted_iota(jnp.int32, (1, LANES), 1)

    def own_rows(ref):
        begin_at = me * share
        row = ref[pl.ds(begin_at // LANES, 1), :]
        part = lax.rem(begin_at, LANES) // share
        spread = row
        for k in range(LANES // share):
            turned = row
            for group in range(LANES // share):
                shift = ((group - k) * share) % LANES
                moved = pltpu.roll(row, shift, 1) if shift else row
                turned = jnp.where(lane // share == group, moved, turned)
            spread = jnp.where(part == k, turned, spread)
        return jnp.concatenate([spread] * (wide // LANES), axis=1)

    group = lax.broadcasted_iota(jnp.int32, (nz, wide), 1) // share
    cos_z = cosines(own_rows(fz_ref), nz, nz)
    first = cos_z.astype(jnp.bfloat16).astype(jnp.float32)
    second = (cos_z - first).astype(jnp.bfloat16).astype(jnp.float32)
    third = cos_z - first - second
    chosen = jnp.where(group == 0, first, jnp.where(group == 1, second, third))
    table[...] = jnp.where(group < 3, chosen, 0.0).astype(jnp.bfloat16)
    cos_x = cosines(own_rows(fx_ref), nx, nx)
    cos_y = cosines(own_rows(fy_ref), ny, ny)
    for x in range(nx):
        weights[x] = cos_x[x : x + 1] * cos_y
    edge = jnp.zeros((ny, nz), jnp.float32)
    for j in range(BASIS):
        vectors[j, 0] = edge
        vectors[j, nx + 1] = edge

    for copy in arriving:
        copy.wait_recv()
    for step in range(1, 4):
        for copy in begin(step):
            copy.wait_recv()

    row_at = lax.broadcasted_iota(jnp.int32, (ny, nz), 0)
    lane_at = lax.broadcasted_iota(jnp.int32, (ny, nz), 1)

    def put_flipped(x, plane):
        turned = plane * sign[x]
        high = turned.astype(jnp.bfloat16)
        flipped[0, x] = high
        flipped[1, x] = (turned - high.astype(jnp.float32)).astype(jnp.bfloat16)

    def sketch_row(j):
        cells = nx * ny
        both = flipped[...].reshape(2 * cells, nz)
        sampled = jnp.dot(both, table[...], preferred_element_type=jnp.float32)
        sampled = (sampled[:cells] + sampled[cells:]) * weights[...].reshape(cells, wide)
        total = jnp.sum(sampled, axis=0, keepdims=True)
        folded = total[:, :LANES]
        for k in range(1, wide // LANES):
            folded = folded + total[:, k * LANES : (k + 1) * LANES]
        spread = folded
        for k in range(1, LANES // share):
            spread = spread + pltpu.roll(folded, k * share, 1)
        rows[pl.ds(j, 1), :] = spread

    small = 0
    for restart in range(ITERS):

        @pl.loop(0, nx)
        def _(x):
            plane = field[x]
            vectors[0, x + 1] = plane
            put_flipped(x, plane)

        sketch_row(BASIS)

        @pl.loop(0, BASIS)
        def _(j):
            before = jnp.maximum(j - 1, 0)
            after = jnp.minimum(j + 1, BASIS - 1)
            step = jnp.where(j == 0, 1.0 / half_range, 2.0 / half_range).astype(jnp.float32)
            old = jnp.where(j == 0, 0.0, 1.0).astype(jnp.float32)

            @pl.loop(0, nx, unroll=2)
            def _(x):
                here = vectors[j, x + 1]
                beside = vectors[j, x + 2] + vectors[j, x]
                beside = beside + jnp.where(row_at < ny - 1, pltpu.roll(here, ny - 1, 0), 0.0)
                beside = beside + jnp.where(row_at > 0, pltpu.roll(here, 1, 0), 0.0)
                beside = beside + jnp.where(lane_at < nz - 1, pltpu.roll(here, nz - 1, 1), 0.0)
                beside = beside + jnp.where(lane_at > 0, pltpu.roll(here, 1, 1), 0.0)
                image = (6.0 + diag[x]) * here - beside
                images[j, x] = image
                put_flipped(x, image)
                turned = (image - center_value * here) * step - old * vectors[before, x + 1]

                @pl.when(j < BASIS - 1)
                def _():
                    vectors[after, x + 1] = turned

            sketch_row(j)

        buffer = sums.at[restart]
        behind = (lane // share == 1) & (lax.broadcasted_iota(jnp.int32, (BASIS, LANES), 0) == 0)
        tile = jnp.where(behind, rows[BASIS : BASIS + 1, :], rows[0:BASIS, :])
        buffer[pl.ds(at["gy"], 1), pl.ds(at["gx"], 1), pl.ds(at["gz"], 1)] = tile.reshape(
            1, 1, 1, BASIS, LANES
        )
        whole = {axis: False for axis in sizes}
        for axis in ("gy", "gx", "gz"):
            here, size = at[axis], sizes[axis]
            arrivals = []
            for k in range(1, size):
                target, origin = lax.rem(here + k, size), lax.rem(here + size - k, size)
                sems = dict(send_sem=small_send.at[small], recv_sem=small_recv.at[small])
                go = dict(device_id={axis: target}, device_id_type=MESH)
                small += 1
                source, landing = (
                    buffer.at[
                        tuple(
                            slice(None) if whole[name] else pl.ds(place[name], 1)
                            for name in ("gy", "gx", "gz")
                        )
                    ]
                    for place in (at, {**at, axis: origin})
                )
                copy = pltpu.make_async_remote_copy(src_ref=source, dst_ref=source, **sems, **go)
                copy.start()
                gather.started.append(copy)
                arrivals.append(
                    pltpu.make_async_remote_copy(src_ref=landing, dst_ref=landing, **sems, **go)
                )
            for copy in arrivals:
                copy.wait_recv()
            whole[axis] = True
        devices = math.prod(sizes.values())
        tiles = buffer[...].reshape(devices, BASIS, LANES)
        sketched = [jnp.where(lane < share, tiles[:, j, :], 0.0) for j in range(BASIS)]
        aside = pltpu.roll(tiles[:, 0, :], LANES - share, 1)
        solved = solve_rows(sketched, jnp.where(lane < share, aside, 0.0))

        kept = (pl.ds(x0 + 1, bx), pl.ds(y0, by), pl.ds(z0, bz))
        total = jnp.zeros((bx, by, bz), jnp.float32) if restart == 0 else sol_ref[...]
        for j in range(BASIS):
            total = total + solved[j].reshape(1, 1, 1) * vectors[(j,) + kept]
        sol_ref[...] = total
        if restart == ITERS - 1:
            left = field[own]
            for j in range(BASIS):
                left = left - solved[j].reshape(1, 1, 1) * images[(j,) + own]
            res_ref[...] = left
        else:
            for copy in gather.started:
                copy.wait_send()
            gather.started = []

            @pl.loop(0, nx)
            def _(x):
                left = field[x]
                for j in range(BASIS):
                    left = left - solved[j] * images[j, x]
                field[x] = left

    for copy in gather.started:
        copy.wait_send()


def whole_fits(sizes, nx, ny, nz, sampled):
    devices = math.prod(sizes.values())
    share = sampled // devices
    if sizes["gy"] % 2 or sampled % devices or share == 0 or LANES % share or 2 * share > LANES:
        return False
    if nz % LANES or nz // sizes["gz"] != LANES or (ny // sizes["gy"]) % 8 or ny % 16:
        return False
    return nx * ny * nz * 4 * (2 * BASIS + 8) <= 24 * 1024 * 1024


def whole_shards(sizes, right_side, diagonal, sign_bits, freq_x, freq_y, freq_z):
    block = right_side.shape
    nx, ny, nz = (size * sizes[axis] for size, axis in zip(block, ("gx", "gy", "gz")))
    share = freq_x.shape[0] // math.prod(sizes.values())
    wide = -(-3 * share // LANES) * LANES
    freqs = [f.reshape(-1, LANES) for f in (freq_x, freq_y, freq_z)]
    f32 = jnp.float32
    copies = copies_needed(sizes)
    smalls = ITERS * sum(size - 1 for size in sizes.values())
    return pl.pallas_call(
        functools.partial(whole_kernel, sizes, share),
        out_shape=[jax.ShapeDtypeStruct(block, f32)] * 2,
        in_specs=[pl.BlockSpec(memory_space=pltpu.VMEM)] * 6,
        out_specs=[pl.BlockSpec(memory_space=pltpu.VMEM)] * 2,
        scratch_shapes=[
            pltpu.VMEM((nx, ny, nz), f32),
            pltpu.VMEM((nx, ny, nz), f32),
            pltpu.VMEM((nx, ny, nz), f32),
            pltpu.VMEM((BASIS, nx + 2, ny, nz), f32),
            pltpu.VMEM((BASIS, nx, ny, nz), f32),
            pltpu.VMEM((2, nx, ny, nz), jnp.bfloat16),
            pltpu.VMEM((nz, wide), jnp.bfloat16),
            pltpu.VMEM((nx, ny, wide), f32),
            pltpu.VMEM((16, LANES), f32),
            pltpu.VMEM((ITERS, sizes["gy"], sizes["gx"], sizes["gz"], BASIS, LANES), f32),
            pltpu.SemaphoreType.DMA((copies,)),
            pltpu.SemaphoreType.DMA((copies,)),
            pltpu.SemaphoreType.DMA((smalls,)),
            pltpu.SemaphoreType.DMA((smalls,)),
        ],
        compiler_params=pltpu.CompilerParams(
            collective_id=0, has_side_effects=True, vmem_limit_bytes=40 * 1024 * 1024
        ),
    )(right_side, diagonal, sign_bits, *freqs)


def solution(mesh):
    in_specs = (P("gx", "gy", "gz"), P("gx", "gy", "gz"), P("gx", "gy", "gz"), P(), P(), P())
    out_specs = (P("gx", "gy", "gz"), P("gx", "gy", "gz"))
    sizes = {axis: mesh.shape[axis] for axis in ("gx", "gy", "gz")}

    def run(right_side, diagonal, sign_bits, freq_x, freq_y, freq_z):
        plan = shards
        if whole_fits(sizes, *right_side.shape, freq_x.shape[0]):
            plan = functools.partial(whole_shards, sizes)
        mapped = jax.shard_map(
            plan, mesh=mesh, in_specs=in_specs, out_specs=out_specs, check_vma=False
        )
        return mapped(right_side, diagonal, sign_bits, freq_x, freq_y, freq_z)

    return run
```

```python
import functools
import math

import jax
import jax.numpy as jnp
from jax import lax
from jax.experimental import pallas as pl
from jax.experimental.pallas import tpu as pltpu
from jax.sharding import PartitionSpec as P

BASIS = 8
ITERS = 2


center_value = 7.0
half_range = 7.0
tiny_value = 1e-06
highest = lax.Precision.HIGHEST


def extended(shard, sides, width):
    for axis, dim in sides:
        size, length = (lax.axis_size(axis), shard.shape[dim])
        up = [(i, (i + 1) % size) for i in range(size - 1)]
        down = [(j, i) for i, j in up]
        last = lax.slice_in_dim(shard, length - width, length, axis=dim)
        first = lax.slice_in_dim(shard, 0, width, axis=dim)
        before = lax.ppermute(last, axis, up)
        after = lax.ppermute(first, axis, down)
        shard = jnp.concatenate([before, shard, after], axis=dim)
    return shard


def stencil(padded, diagonal):
    beside = padded[2:, 1:-1, 1:-1] + padded[:-2, 1:-1, 1:-1]
    beside = beside + padded[1:-1, 2:, 1:-1] + padded[1:-1, :-2, 1:-1]
    beside = beside + padded[1:-1, 1:-1, 2:] + padded[1:-1, 1:-1, :-2]
    return (6.0 + diagonal) * padded[1:-1, 1:-1, 1:-1] - beside


def cosine_table(freqs, offset, count, length):
    indices = offset + jnp.arange(count, dtype=jnp.int32)
    phases = (2 * indices[:, None] + 1) * freqs[None, :] % (4 * length)
    return (jnp.sqrt(2.0 / length) * jnp.cos(jnp.pi * phases / (2.0 * length))).astype(jnp.float32)


def least_squares(matrix):
    count = matrix.shape[0] - 1
    target = matrix[count]
    orthonormal = []
    upper = {}
    for column_at in range(count):
        column = matrix[column_at]
        for repeat in range(2):
            for earlier in range(column_at):
                amount = jnp.dot(orthonormal[earlier], column, precision=highest)
                column = column - amount * orthonormal[earlier]
                upper[earlier, column_at] = upper.get((earlier, column_at), 0.0) + amount
        length = jnp.sqrt(jnp.dot(column, column, precision=highest) + tiny_value)
        orthonormal.append(column / length)
        upper[column_at, column_at] = length
    projected = [jnp.dot(basis_row, target, precision=highest) for basis_row in orthonormal]
    solved = [None] * count
    for row_at in range(count - 1, -1, -1):
        value = projected[row_at]
        for later in range(row_at + 1, count):
            value = value - upper[row_at, later] * solved[later]
        solved[row_at] = value / upper[row_at, row_at]
    return jnp.stack(solved)


def basis_plain(residual, diagonal):
    vectors = [residual]
    images = []
    for position in range(BASIS):
        padded = extended(vectors[position], (("gx", 0), ("gy", 1), ("gz", 2)), 1)
        image = stencil(padded, diagonal)
        images.append(image)
        if position + 1 < BASIS:
            turned = (image - center_value * vectors[position]) / half_range
            vectors.append(turned if position == 0 else 2.0 * turned - vectors[position - 1])
    return (vectors, images)


def local_sketch(columns, signs, table_x, table_y, table_z):
    flipped = jnp.stack(columns, axis=2) * signs[:, :, None, :]
    size_x, size_y, count, depth = flipped.shape
    rows_flat = flipped.reshape(-1, depth)
    weights = table_x[:, None, :] * table_y[None, :, :]
    sampled = table_z.shape[1]
    block = min(512, sampled)
    pieces = []
    for begin in range(0, sampled, block):
        inner_sums = jnp.dot(
            rows_flat,
            table_z[:, begin : begin + block],
            precision=highest,
            preferred_element_type=jnp.float32,
        )
        inner_sums = inner_sums.reshape(size_x, size_y, count, block)
        pieces.append(
            jnp.einsum(
                "xyjs,xys->js", inner_sums, weights[:, :, begin : begin + block], precision=highest
            )
        )
    return jnp.concatenate(pieces, axis=1)


def shards(right_side, diagonal, sign_bits, freq_x, freq_y, freq_z):
    size_x, size_y, size_z = right_side.shape
    table_x = cosine_table(
        freq_x, lax.axis_index("gx") * size_x, size_x, size_x * lax.axis_size("gx")
    )
    table_y = cosine_table(
        freq_y, lax.axis_index("gy") * size_y, size_y, size_y * lax.axis_size("gy")
    )
    table_z = cosine_table(
        freq_z, lax.axis_index("gz") * size_z, size_z, size_z * lax.axis_size("gz")
    )
    signs = 1.0 - 2.0 * sign_bits.astype(jnp.float32)
    solution = jnp.zeros_like(right_side)
    residual = right_side
    for restart in range(ITERS):
        vectors, images = basis_plain(residual, diagonal)
        partial_value = local_sketch(images + [residual], signs, table_x, table_y, table_z)
        shares = lax.psum_scatter(partial_value, "gx", scatter_dimension=1, tiled=True)
        shares = lax.psum(shares, ("gy", "gz"))
        matrix = lax.all_gather(shares, "gx", axis=1, tiled=True)
        weights_solved = least_squares(matrix)
        for position in range(BASIS):
            solution = solution + weights_solved[position] * vectors[position]
            residual = residual - weights_solved[position] * images[position]
    return (solution, residual)


MESH = pl.DeviceIdType.MESH
LANES = 128
SINE = [(-1.0) ** k / math.factorial(2 * k + 1) for k in range(7)]


def cosines(freqs, count, length):
    cells = lax.broadcasted_iota(jnp.int32, (count, freqs.shape[1]), 0)
    phases = lax.rem((2 * cells + 1) * freqs, 4 * length)
    folded = length - jnp.minimum(phases, 4 * length - phases)
    angle = folded.astype(jnp.float32) * (math.pi / (2.0 * length))
    square = angle * angle
    value = jnp.full_like(angle, SINE[-1])
    for term in SINE[-2::-1]:
        value = value * square + term
    return value * angle * math.sqrt(2.0 / length)


def total_of(value):
    return jnp.sum(jnp.sum(value, axis=0, keepdims=True), axis=1, keepdims=True)


def solve_rows(rows, target):
    count = len(rows)
    basis, among, short, upper, inverse = [], [], [], {}, []
    for at_column in range(count):
        column = rows[at_column]
        for repeat in range(2):
            left = [total_of(q * column) for q in basis]
            amounts = []
            for e in range(at_column):
                amount = left[e]
                amounts.append(amount)
                left[e] = amount * short[e]
                for f in range(at_column):
                    if f != e:
                        left[f] = left[f] - amount * among[max(e, f)][min(e, f)]
            for e in range(at_column):
                column = column - amounts[e] * basis[e]
                upper[e, at_column] = upper.get((e, at_column), 0.0) + amounts[e]
        length = jnp.sqrt(total_of(column * column) + tiny_value)
        scale = 1.0 / length
        basis.append(column * scale)
        among.append([value * scale for value in left] if at_column else [])
        short.append(tiny_value * scale * scale)
        inverse.append(scale)
    projected = [total_of(q * target) for q in basis]
    solved = [None] * count
    for row in range(count - 1, -1, -1):
        value = projected[row]
        for later in range(row + 1, count):
            value = value - upper[row, later] * solved[later]
        solved[row] = value * inverse[row]
    return solved


class Gather:
    def __init__(self, sizes, block, send_sem, recv_sem):
        self.sizes, self.block = sizes, block
        self.send_sem, self.recv_sem = send_sem, recv_sem
        self.count = 0
        self.at = {axis: lax.axis_index(axis) for axis in sizes}

    def regions(self, ref, state, at):
        bx, by, bz = self.block
        gx, gy, gz = at["gx"], at["gy"], at["gz"]
        xs = slice(None) if state["x"] == "all" else pl.ds(gx * bx, bx)
        zs = slice(None) if state["z"] == "all" else pl.ds(pl.multiple_of(gz * bz, bz), bz)
        if state["y"] == "own":
            ys = [gy]
        else:
            ys = [lax.rem(gy, 2) + 2 * k for k in range(self.sizes["gy"] // 2)]
        return [ref.at[xs, pl.ds(pl.multiple_of(y * by, by), by), zs] for y in ys]

    def plan(self, ref, state, phase):
        axis = {"X": "gx", "Z": "gz", "H": "gy", "C": "gy"}[phase]
        size, here = self.sizes[axis], self.at[axis]
        if phase == "C":
            hops = [(here + 1 - 2 * lax.rem(here, 2), here + 1 - 2 * lax.rem(here, 2))]
        else:
            stride = 2 if phase == "H" else 1
            hops = [
                (lax.rem(here + k, size), lax.rem(here + size - k, size))
                for k in range(stride, size, stride)
            ]
        sends, arriving = [], []
        for target, origin in hops:
            mine = self.regions(ref, state, self.at)
            theirs = self.regions(ref, state, {**self.at, axis: origin})
            for source, landing in zip(mine, theirs):
                n = self.count
                self.count += 1
                sems = dict(send_sem=self.send_sem.at[n], recv_sem=self.recv_sem.at[n])
                go = dict(device_id={axis: target}, device_id_type=MESH)
                sends.append(
                    pltpu.make_async_remote_copy(src_ref=source, dst_ref=source, **sems, **go)
                )
                arriving.append(
                    pltpu.make_async_remote_copy(src_ref=landing, dst_ref=landing, **sems, **go)
                )
        if phase == "X":
            state["x"] = "all"
        elif phase == "Z":
            state["z"] = "all"
        elif phase == "H":
            state["y"] = "half"
        else:
            state["y"] = "all"
        return sends, arriving


def copies_needed(sizes):
    half = sizes["gy"] // 2
    return 3 * (sizes["gx"] - 1 + (sizes["gz"] - 1) * half + half - 1 + half) + 8


def whole_kernel(
    sizes, share, right_ref, diagonal_ref, bits_ref, fx_ref, fy_ref, fz_ref, sol_ref, res_ref,
    images, diag, sign, vectors, table, weights, rows, sums, bits, freqs, load_sem, send_sem,
    recv_sem, small_send, small_recv,
):
    bx, by, bz = right_ref.shape
    _, nx, ny, nz = images.shape
    wide = table.shape[1]
    cells = nx * ny
    at = {axis: lax.axis_index(axis) for axis in sizes}
    x0 = at["gx"] * bx
    y0 = pl.multiple_of(at["gy"] * by, by)
    z0 = pl.multiple_of(at["gz"] * bz, bz)
    own = (pl.ds(x0, bx), pl.ds(y0, by), pl.ds(z0, bz))
    field = images.at[BASIS]

    loads = [
        pltpu.make_async_copy(source, target, load_sem.at[n])
        for n, (source, target) in enumerate(
            [
                (right_ref, field.at[own]),
                (diagonal_ref, diag.at[own]),
                (bits_ref, bits),
                (fx_ref, freqs.at[0]),
                (fy_ref, freqs.at[1]),
                (fz_ref, freqs.at[2]),
            ]
        )
    ]
    for copy in loads:
        copy.start()
    barrier = pltpu.get_barrier_semaphore()
    peers = 0
    for axis, size in sizes.items():
        for k in range(1, size):
            target = lax.rem(at[axis] + k, size)
            pl.semaphore_signal(barrier, inc=1, device_id={axis: target}, device_id_type=MESH)
            peers += 1

    gather = Gather(sizes, (bx, by, bz), send_sem, recv_sem)
    plans = []
    for ref, order in [(field, "XZHC"), (diag, "XHZC"), (sign, "XZHC")]:
        state = {"x": "own", "y": "own", "z": "own"}
        plans.append([gather.plan(ref, state, phase) for phase in order])

    def begin(array, step):
        for copy in plans[array][step][0]:
            copy.start()

    def arrive(array, step):
        for copy in plans[array][step][1]:
            copy.wait_recv()

    for copy in loads[:2]:
        copy.wait()
    pl.semaphore_wait(barrier, peers)
    begin(0, 0)
    begin(1, 0)
    for copy in loads[2:]:
        copy.wait()
    sol_ref[...] = jnp.zeros_like(sol_ref)
    sign[own] = 1.0 - 2.0 * bits[...].astype(jnp.float32)
    begin(2, 0)

    me = (at["gx"] * sizes["gy"] + at["gy"]) * sizes["gz"] + at["gz"]
    lane = lax.broadcasted_iota(jnp.int32, (1, LANES), 1)

    def own_rows(number):
        begin_at = me * share
        row = freqs[number, pl.ds(begin_at // LANES, 1), :]
        part = lax.rem(begin_at, LANES) // share
        spread = row
        for k in range(LANES // share):
            turned = row
            for group in range(LANES // share):
                shift = ((group - k) * share) % LANES
                moved = pltpu.roll(row, shift, 1) if shift else row
                turned = jnp.where(lane // share == group, moved, turned)
            spread = jnp.where(part == k, turned, spread)
        return jnp.concatenate([spread] * (wide // LANES), axis=1)

    def tables():
        cos_x = cosines(own_rows(0), nx, nx)
        cos_y = cosines(own_rows(1), ny, ny)
        for x in range(nx):
            weights[x] = cos_x[x : x + 1] * cos_y
        group = lax.broadcasted_iota(jnp.int32, (nz, wide), 1) // share
        cos_z = cosines(own_rows(2), nz, nz)
        first = cos_z.astype(jnp.bfloat16).astype(jnp.float32)
        second = (cos_z - first).astype(jnp.bfloat16).astype(jnp.float32)
        third = cos_z - first - second
        chosen = jnp.where(group == 0, first, jnp.where(group == 1, second, third))
        table[...] = jnp.where(group < 3, chosen, 0.0).astype(jnp.bfloat16)

    for step in range(1, 4):
        for array in range(2):
            arrive(array, step - 1)
            begin(array, step)
        if step == 1:
            tables()
    arrive(0, 3)
    arrive(1, 3)

    row_at = lax.broadcasted_iota(jnp.int32, (ny, nz), 0)
    lane_at = lax.broadcasted_iota(jnp.int32, (ny, nz), 1)

    def vector(j):
        return field if j == 0 else vectors.at[j - 1]

    def stencil_step(j):
        here_ref = vector(j)
        for x in range(nx):
            here = here_ref[x]
            beside = None
            for near in (x + 1, x - 1):
                if 0 <= near < nx:
                    beside = here_ref[near] if beside is None else beside + here_ref[near]
            beside = beside + jnp.where(row_at < ny - 1, pltpu.roll(here, ny - 1, 0), 0.0)
            beside = beside + jnp.where(row_at > 0, pltpu.roll(here, 1, 0), 0.0)
            beside = beside + jnp.where(lane_at < nz - 1, pltpu.roll(here, nz - 1, 1), 0.0)
            beside = beside + jnp.where(lane_at > 0, pltpu.roll(here, 1, 1), 0.0)
            image = (6.0 + diag[x]) * here - beside
            images[j, x] = image
            if j + 1 < BASIS:
                turned = image - center_value * here
                if j == 0:
                    vectors[j, x] = turned * (1.0 / half_range)
                else:
                    vectors[j, x] = turned * (2.0 / half_range) - vector(j - 1)[x]

    def sketch_row(j):
        turned = (images[j] * sign[...]).reshape(cells, nz)
        high = turned.astype(jnp.bfloat16)
        low = (turned - high.astype(jnp.float32)).astype(jnp.bfloat16)
        both = jnp.concatenate([high, low], axis=0)
        sampled = jnp.dot(both, table[...], preferred_element_type=jnp.float32)
        sampled = (sampled[:cells] + sampled[cells:]) * weights[...].reshape(cells, wide)
        total = jnp.sum(sampled, axis=0, keepdims=True)
        folded = total[:, :LANES]
        for k in range(1, wide // LANES):
            folded = folded + total[:, k * LANES : (k + 1) * LANES]
        spread = folded
        for k in range(1, LANES // share):
            spread = spread + pltpu.roll(folded, k * share, 1)
        rows[pl.ds(j, 1), :] = spread

    @pl.loop(0, ITERS)
    def _(restart):
        for j in range(BASIS):
            stencil_step(j)
            if j in (1, 3, 5):

                @pl.when(restart == 0)
                def _():
                    arrive(2, j // 2)
                    begin(2, j // 2 + 1)

        @pl.when(restart == 0)
        def _():
            arrive(2, 3)

        @pl.loop(0, BASIS + 1, unroll=3)
        def _(j):
            sketch_row(j)

        buffer = sums.at[restart]
        behind = (lane // share == 1) & (lax.broadcasted_iota(jnp.int32, (BASIS, LANES), 0) == 0)
        tile = jnp.where(behind, rows[BASIS : BASIS + 1, :], rows[0:BASIS, :])
        buffer[pl.ds(at["gy"], 1), pl.ds(at["gx"], 1), pl.ds(at["gz"], 1)] = tile.reshape(
            1, 1, 1, BASIS, LANES
        )
        whole = {axis: False for axis in sizes}
        small = restart * sum(size - 1 for size in sizes.values())
        started = []
        for axis in ("gy", "gx", "gz"):
            here, size = at[axis], sizes[axis]
            arrivals = []
            for k in range(1, size):
                target, origin = lax.rem(here + k, size), lax.rem(here + size - k, size)
                sems = dict(send_sem=small_send.at[small], recv_sem=small_recv.at[small])
                go = dict(device_id={axis: target}, device_id_type=MESH)
                small = small + 1
                source, landing = (
                    buffer.at[
                        tuple(
                            slice(None) if whole[name] else pl.ds(place[name], 1)
                            for name in ("gy", "gx", "gz")
                        )
                    ]
                    for place in (at, {**at, axis: origin})
                )
                copy = pltpu.make_async_remote_copy(src_ref=source, dst_ref=source, **sems, **go)
                copy.start()
                started.append(copy)
                arrivals.append(
                    pltpu.make_async_remote_copy(src_ref=landing, dst_ref=landing, **sems, **go)
                )
            for copy in arrivals:
                copy.wait_recv()
            whole[axis] = True
        devices = math.prod(sizes.values())
        tiles = buffer[...].reshape(devices, BASIS, LANES)
        sketched = [jnp.where(lane < share, tiles[:, j, :], 0.0) for j in range(BASIS)]
        aside = pltpu.roll(tiles[:, 0, :], LANES - share, 1)
        solved = solve_rows(sketched, jnp.where(lane < share, aside, 0.0))
        for copy in started:
            copy.wait_send()

        total = sol_ref[...]
        for j in range(BASIS):
            total = total + solved[j].reshape(1, 1, 1) * vector(j)[own]
        sol_ref[...] = total

        @pl.when(restart == 0)
        def _():
            for plan in plans:
                for sends, _ in plan:
                    for copy in sends:
                        copy.wait_send()

        @pl.when(restart == ITERS - 1)
        def _():
            left = field[own]
            for j in range(BASIS):
                left = left - solved[j].reshape(1, 1, 1) * images[(j,) + own]
            res_ref[...] = left

        @pl.when(restart < ITERS - 1)
        def _():
            for x in range(nx):
                left = field[x]
                for j in range(BASIS):
                    left = left - solved[j] * images[j, x]
                field[x] = left


def whole_fits(sizes, nx, ny, nz, sampled):
    devices = math.prod(sizes.values())
    share = sampled // devices
    if sizes["gy"] % 2 or sampled % devices or share == 0 or LANES % share or 2 * share > LANES:
        return False
    if nz % LANES or nz // sizes["gz"] != LANES or (ny // sizes["gy"]) % 8 or ny % 16:
        return False
    return nx * ny * nz * 4 * (2 * BASIS + 8) <= 24 * 1024 * 1024


def whole_shards(sizes, right_side, diagonal, sign_bits, freq_x, freq_y, freq_z):
    block = right_side.shape
    nx, ny, nz = (size * sizes[axis] for size, axis in zip(block, ("gx", "gy", "gz")))
    share = freq_x.shape[0] // math.prod(sizes.values())
    wide = -(-3 * share // LANES) * LANES
    freqs = [f.reshape(-1, LANES) for f in (freq_x, freq_y, freq_z)]
    f32 = jnp.float32
    copies = copies_needed(sizes)
    smalls = ITERS * sum(size - 1 for size in sizes.values())
    return pl.pallas_call(
        functools.partial(whole_kernel, sizes, share),
        out_shape=[jax.ShapeDtypeStruct(block, f32)] * 2,
        in_specs=[pl.BlockSpec(memory_space=pl.ANY)] * 6,
        out_specs=[pl.BlockSpec(memory_space=pltpu.VMEM)] * 2,
        scratch_shapes=[
            pltpu.VMEM((BASIS + 1, nx, ny, nz), f32),
            pltpu.VMEM((nx, ny, nz), f32),
            pltpu.VMEM((nx, ny, nz), f32),
            pltpu.VMEM((BASIS - 1, nx, ny, nz), f32),
            pltpu.VMEM((nz, wide), jnp.bfloat16),
            pltpu.VMEM((nx, ny, wide), f32),
            pltpu.VMEM((16, LANES), f32),
            pltpu.VMEM((ITERS, sizes["gy"], sizes["gx"], sizes["gz"], BASIS, LANES), f32),
            pltpu.VMEM(block, jnp.int32),
            pltpu.VMEM((3,) + freqs[0].shape, jnp.int32),
            pltpu.SemaphoreType.DMA((6,)),
            pltpu.SemaphoreType.DMA((copies,)),
            pltpu.SemaphoreType.DMA((copies,)),
            pltpu.SemaphoreType.DMA((smalls,)),
            pltpu.SemaphoreType.DMA((smalls,)),
        ],
        compiler_params=pltpu.CompilerParams(
            collective_id=0, has_side_effects=True, vmem_limit_bytes=40 * 1024 * 1024
        ),
    )(right_side, diagonal, sign_bits, *freqs)


def solution(mesh):
    in_specs = (P("gx", "gy", "gz"), P("gx", "gy", "gz"), P("gx", "gy", "gz"), P(), P(), P())
    out_specs = (P("gx", "gy", "gz"), P("gx", "gy", "gz"))
    sizes = {axis: mesh.shape[axis] for axis in ("gx", "gy", "gz")}

    def run(right_side, diagonal, sign_bits, freq_x, freq_y, freq_z):
        plan = shards
        if whole_fits(sizes, *right_side.shape, freq_x.shape[0]):
            plan = functools.partial(whole_shards, sizes)
        mapped = jax.shard_map(
            plan, mesh=mesh, in_specs=in_specs, out_specs=out_specs, check_vma=False
        )
        return mapped(right_side, diagonal, sign_bits, freq_x, freq_y, freq_z)

    return run
```

```python
import functools
import math

import jax
import jax.numpy as jnp
from jax import lax
from jax.experimental import pallas as pl
from jax.experimental.pallas import tpu as pltpu
from jax.sharding import PartitionSpec as P

BASIS = 8
ITERS = 2


center_value = 7.0
half_range = 7.0
tiny_value = 1e-06
highest = lax.Precision.HIGHEST


def extended(shard, sides, width):
    for axis, dim in sides:
        size, length = (lax.axis_size(axis), shard.shape[dim])
        up = [(i, (i + 1) % size) for i in range(size - 1)]
        down = [(j, i) for i, j in up]
        last = lax.slice_in_dim(shard, length - width, length, axis=dim)
        first = lax.slice_in_dim(shard, 0, width, axis=dim)
        before = lax.ppermute(last, axis, up)
        after = lax.ppermute(first, axis, down)
        shard = jnp.concatenate([before, shard, after], axis=dim)
    return shard


def stencil(padded, diagonal):
    beside = padded[2:, 1:-1, 1:-1] + padded[:-2, 1:-1, 1:-1]
    beside = beside + padded[1:-1, 2:, 1:-1] + padded[1:-1, :-2, 1:-1]
    beside = beside + padded[1:-1, 1:-1, 2:] + padded[1:-1, 1:-1, :-2]
    return (6.0 + diagonal) * padded[1:-1, 1:-1, 1:-1] - beside


def cosine_table(freqs, offset, count, length):
    indices = offset + jnp.arange(count, dtype=jnp.int32)
    phases = (2 * indices[:, None] + 1) * freqs[None, :] % (4 * length)
    return (jnp.sqrt(2.0 / length) * jnp.cos(jnp.pi * phases / (2.0 * length))).astype(jnp.float32)


def least_squares(matrix):
    count = matrix.shape[0] - 1
    target = matrix[count]
    orthonormal = []
    upper = {}
    for column_at in range(count):
        column = matrix[column_at]
        for repeat in range(2):
            for earlier in range(column_at):
                amount = jnp.dot(orthonormal[earlier], column, precision=highest)
                column = column - amount * orthonormal[earlier]
                upper[earlier, column_at] = upper.get((earlier, column_at), 0.0) + amount
        length = jnp.sqrt(jnp.dot(column, column, precision=highest) + tiny_value)
        orthonormal.append(column / length)
        upper[column_at, column_at] = length
    projected = [jnp.dot(basis_row, target, precision=highest) for basis_row in orthonormal]
    solved = [None] * count
    for row_at in range(count - 1, -1, -1):
        value = projected[row_at]
        for later in range(row_at + 1, count):
            value = value - upper[row_at, later] * solved[later]
        solved[row_at] = value / upper[row_at, row_at]
    return jnp.stack(solved)


def basis_plain(residual, diagonal):
    vectors = [residual]
    images = []
    for position in range(BASIS):
        padded = extended(vectors[position], (("gx", 0), ("gy", 1), ("gz", 2)), 1)
        image = stencil(padded, diagonal)
        images.append(image)
        if position + 1 < BASIS:
            turned = (image - center_value * vectors[position]) / half_range
            vectors.append(turned if position == 0 else 2.0 * turned - vectors[position - 1])
    return (vectors, images)


def local_sketch(columns, signs, table_x, table_y, table_z):
    flipped = jnp.stack(columns, axis=2) * signs[:, :, None, :]
    size_x, size_y, count, depth = flipped.shape
    rows_flat = flipped.reshape(-1, depth)
    weights = table_x[:, None, :] * table_y[None, :, :]
    sampled = table_z.shape[1]
    block = min(512, sampled)
    pieces = []
    for begin in range(0, sampled, block):
        inner_sums = jnp.dot(
            rows_flat,
            table_z[:, begin : begin + block],
            precision=highest,
            preferred_element_type=jnp.float32,
        )
        inner_sums = inner_sums.reshape(size_x, size_y, count, block)
        pieces.append(
            jnp.einsum(
                "xyjs,xys->js", inner_sums, weights[:, :, begin : begin + block], precision=highest
            )
        )
    return jnp.concatenate(pieces, axis=1)


def shards(right_side, diagonal, sign_bits, freq_x, freq_y, freq_z):
    size_x, size_y, size_z = right_side.shape
    table_x = cosine_table(
        freq_x, lax.axis_index("gx") * size_x, size_x, size_x * lax.axis_size("gx")
    )
    table_y = cosine_table(
        freq_y, lax.axis_index("gy") * size_y, size_y, size_y * lax.axis_size("gy")
    )
    table_z = cosine_table(
        freq_z, lax.axis_index("gz") * size_z, size_z, size_z * lax.axis_size("gz")
    )
    signs = 1.0 - 2.0 * sign_bits.astype(jnp.float32)
    solution = jnp.zeros_like(right_side)
    residual = right_side
    for restart in range(ITERS):
        vectors, images = basis_plain(residual, diagonal)
        partial_value = local_sketch(images + [residual], signs, table_x, table_y, table_z)
        shares = lax.psum_scatter(partial_value, "gx", scatter_dimension=1, tiled=True)
        shares = lax.psum(shares, ("gy", "gz"))
        matrix = lax.all_gather(shares, "gx", axis=1, tiled=True)
        weights_solved = least_squares(matrix)
        for position in range(BASIS):
            solution = solution + weights_solved[position] * vectors[position]
            residual = residual - weights_solved[position] * images[position]
    return (solution, residual)


MESH = pl.DeviceIdType.MESH
LANES = 128
SINE = [(-1.0) ** k / math.factorial(2 * k + 1) for k in range(7)]


def cosines(freqs, count, length):
    cells = lax.broadcasted_iota(jnp.int32, (count, freqs.shape[1]), 0)
    phases = lax.rem((2 * cells + 1) * freqs, 4 * length)
    folded = length - jnp.minimum(phases, 4 * length - phases)
    angle = folded.astype(jnp.float32) * (math.pi / (2.0 * length))
    square = angle * angle
    value = jnp.full_like(angle, SINE[-1])
    for term in SINE[-2::-1]:
        value = value * square + term
    return value * angle * math.sqrt(2.0 / length)


def total_of(value):
    return jnp.sum(jnp.sum(value, axis=0, keepdims=True), axis=1, keepdims=True)


def swept(left, among, short):
    count, left, amounts = len(left), list(left), []
    for e in range(count):
        amount = left[e]
        amounts.append(amount)
        left[e] = amount * short[e]
        for f in range(count):
            if f != e:
                left[f] = left[f] - amount * among[max(e, f)][min(e, f)]
    return amounts, left


def solve_rows(rows, target):
    count = len(rows)
    inner = [[total_of(rows[i] * rows[j]) for j in range(i, count)] for i in range(count)]
    basis, onto, among, short, upper, inverse = [], [], [], [], {}, []
    for at_column in range(count):
        column, square, left = rows[at_column], inner[at_column][0], []
        amounts = [0.0] * at_column
        if at_column:
            first, _ = swept([onto[e][at_column] for e in range(at_column)], among, short)
            for e in range(at_column):
                column = column - first[e] * basis[e]
            start = [total_of(q * column) for q in basis]
            square = total_of(column * column)
            second, left = swept(start, among, short)
            for e in range(at_column):
                column = column - second[e] * basis[e]
                square = square - second[e] * (start[e] + left[e])
                amounts[e] = first[e] + second[e]
                upper[e, at_column] = amounts[e]
        scale = lax.rsqrt(jnp.maximum(square, 0.0) + tiny_value)
        basis.append(column * scale)
        along = {}
        for j in range(at_column + 1, count):
            value = inner[at_column][j - at_column]
            for e in range(at_column):
                value = value - amounts[e] * onto[e][j]
            along[j] = value * scale
        onto.append(along)
        among.append([value * scale for value in left])
        short.append(tiny_value * scale * scale)
        inverse.append(scale)
    projected = [total_of(q * target) for q in basis]
    solved = [None] * count
    for row in range(count - 1, -1, -1):
        value = projected[row]
        for later in range(row + 1, count):
            value = value - upper[row, later] * solved[later]
        solved[row] = value * inverse[row]
    return solved


class Gather:
    def __init__(self, sizes, block, send_sem, recv_sem):
        self.sizes, self.block = sizes, block
        self.send_sem, self.recv_sem = send_sem, recv_sem
        self.count = 0
        self.at = {axis: lax.axis_index(axis) for axis in sizes}

    def regions(self, ref, state, at):
        bx, by, bz = self.block
        gx, gy, gz = at["gx"], at["gy"], at["gz"]
        xs = slice(None) if state["x"] == "all" else pl.ds(gx * bx, bx)
        zs = slice(None) if state["z"] == "all" else pl.ds(pl.multiple_of(gz * bz, bz), bz)
        if state["y"] == "own":
            ys = [gy]
        else:
            ys = [lax.rem(gy, 2) + 2 * k for k in range(self.sizes["gy"] // 2)]
        return [ref.at[xs, pl.ds(pl.multiple_of(y * by, by), by), zs] for y in ys]

    def plan(self, ref, state, phase):
        axis = {"X": "gx", "Z": "gz", "H": "gy", "C": "gy"}[phase]
        size, here = self.sizes[axis], self.at[axis]
        if phase == "C":
            hops = [(here + 1 - 2 * lax.rem(here, 2), here + 1 - 2 * lax.rem(here, 2))]
        else:
            stride = 2 if phase == "H" else 1
            hops = [
                (lax.rem(here + k, size), lax.rem(here + size - k, size))
                for k in range(stride, size, stride)
            ]
        sends, arriving = [], []
        for target, origin in hops:
            mine = self.regions(ref, state, self.at)
            theirs = self.regions(ref, state, {**self.at, axis: origin})
            for source, landing in zip(mine, theirs):
                n = self.count
                self.count += 1
                sems = dict(send_sem=self.send_sem.at[n], recv_sem=self.recv_sem.at[n])
                go = dict(device_id={axis: target}, device_id_type=MESH)
                sends.append(
                    pltpu.make_async_remote_copy(src_ref=source, dst_ref=source, **sems, **go)
                )
                arriving.append(
                    pltpu.make_async_remote_copy(src_ref=landing, dst_ref=landing, **sems, **go)
                )
        if phase == "X":
            state["x"] = "all"
        elif phase == "Z":
            state["z"] = "all"
        elif phase == "H":
            state["y"] = "half"
        else:
            state["y"] = "all"
        return sends, arriving


def copies_needed(sizes):
    half = sizes["gy"] // 2
    return 3 * (sizes["gx"] - 1 + (sizes["gz"] - 1) * half + half - 1 + half) + 8


def whole_kernel(
    sizes, share, right_ref, diagonal_ref, bits_ref, fx_ref, fy_ref, fz_ref, sol_ref, res_ref,
    images, diag, sign, vectors, table, weights, rows, sums, bits, freqs, load_sem, send_sem,
    recv_sem, small_send, small_recv,
):
    bx, by, bz = right_ref.shape
    _, nx, ny, nz = images.shape
    wide = table.shape[1]
    cells = nx * ny
    at = {axis: lax.axis_index(axis) for axis in sizes}
    x0 = at["gx"] * bx
    y0 = pl.multiple_of(at["gy"] * by, by)
    z0 = pl.multiple_of(at["gz"] * bz, bz)
    own = (pl.ds(x0, bx), pl.ds(y0, by), pl.ds(z0, bz))
    field = images.at[BASIS]

    loads = [
        pltpu.make_async_copy(source, target, load_sem.at[n])
        for n, (source, target) in enumerate(
            [
                (right_ref, field.at[own]),
                (diagonal_ref, diag.at[own]),
                (bits_ref, bits),
                (fx_ref, freqs.at[0]),
                (fy_ref, freqs.at[1]),
                (fz_ref, freqs.at[2]),
            ]
        )
    ]
    for copy in loads:
        copy.start()
    barrier = pltpu.get_barrier_semaphore()
    side = sizes["gy"] * sizes["gz"]
    across = at["gy"] * sizes["gz"] + at["gz"]

    def member(index):
        return {"gy": lax.div(index, sizes["gz"]), "gz": lax.rem(index, sizes["gz"])}

    plane_hops = [
        (member(lax.rem(across + k, side)), member(lax.rem(across + side - k, side)))
        for k in range(1, side)
    ]
    line_hops = [
        (
            {"gx": lax.rem(at["gx"] + k, sizes["gx"])},
            {"gx": lax.rem(at["gx"] + sizes["gx"] - k, sizes["gx"])},
        )
        for k in range(1, sizes["gx"])
    ]
    for target, _ in plane_hops + line_hops:
        pl.semaphore_signal(barrier, inc=1, device_id=target, device_id_type=MESH)
    peers = len(plane_hops + line_hops)

    gather = Gather(sizes, (bx, by, bz), send_sem, recv_sem)
    plans = []
    for ref, order in [(field, "XZHC"), (diag, "XHZC"), (sign, "XZHC")]:
        state = {"x": "own", "y": "own", "z": "own"}
        plans.append([gather.plan(ref, state, phase) for phase in order])

    def begin(array, step):
        for copy in plans[array][step][0]:
            copy.start()

    def arrive(array, step):
        for copy in plans[array][step][1]:
            copy.wait_recv()

    for copy in loads[:2]:
        copy.wait()
    pl.semaphore_wait(barrier, peers)
    begin(0, 0)
    begin(1, 0)
    for copy in loads[2:]:
        copy.wait()
    sol_ref[...] = jnp.zeros_like(sol_ref)
    sign[own] = 1.0 - 2.0 * bits[...].astype(jnp.float32)
    begin(2, 0)

    me = (at["gx"] * sizes["gy"] + at["gy"]) * sizes["gz"] + at["gz"]
    lane = lax.broadcasted_iota(jnp.int32, (1, LANES), 1)

    def own_rows(number):
        begin_at = me * share
        row = freqs[number, pl.ds(begin_at // LANES, 1), :]
        part = lax.rem(begin_at, LANES) // share
        spread = row
        for k in range(LANES // share):
            turned = row
            for group in range(LANES // share):
                shift = ((group - k) * share) % LANES
                moved = pltpu.roll(row, shift, 1) if shift else row
                turned = jnp.where(lane // share == group, moved, turned)
            spread = jnp.where(part == k, turned, spread)
        return jnp.concatenate([spread] * (wide // LANES), axis=1)

    def tables():
        cos_x = cosines(own_rows(0), nx, nx)
        cos_y = cosines(own_rows(1), ny, ny)
        for x in range(nx):
            weights[x] = cos_x[x : x + 1] * cos_y
        group = lax.broadcasted_iota(jnp.int32, (nz, wide), 1) // share
        cos_z = cosines(own_rows(2), nz, nz)
        first = cos_z.astype(jnp.bfloat16).astype(jnp.float32)
        second = (cos_z - first).astype(jnp.bfloat16).astype(jnp.float32)
        third = cos_z - first - second
        chosen = jnp.where(group == 0, first, jnp.where(group == 1, second, third))
        table[...] = jnp.where(group < 3, chosen, 0.0).astype(jnp.bfloat16)

    for step in range(1, 4):
        for array in range(2):
            arrive(array, step - 1)
            begin(array, step)
        if step == 1:
            tables()
    arrive(0, 3)
    arrive(1, 3)

    row_at = lax.broadcasted_iota(jnp.int32, (ny, nz), 0)
    lane_at = lax.broadcasted_iota(jnp.int32, (ny, nz), 1)

    def vector(j):
        return field if j == 0 else vectors.at[j - 1]

    def stencil_step(j):
        here_ref = vector(j)
        for x in range(nx):
            here = here_ref[x]
            beside = None
            for near in (x + 1, x - 1):
                if 0 <= near < nx:
                    beside = here_ref[near] if beside is None else beside + here_ref[near]
            beside = beside + jnp.where(row_at < ny - 1, pltpu.roll(here, ny - 1, 0), 0.0)
            beside = beside + jnp.where(row_at > 0, pltpu.roll(here, 1, 0), 0.0)
            beside = beside + jnp.where(lane_at < nz - 1, pltpu.roll(here, nz - 1, 1), 0.0)
            beside = beside + jnp.where(lane_at > 0, pltpu.roll(here, 1, 1), 0.0)
            image = (6.0 + diag[x]) * here - beside
            images[j, x] = image
            if j + 1 < BASIS:
                turned = image - center_value * here
                if j == 0:
                    vectors[j, x] = turned * (1.0 / half_range)
                else:
                    vectors[j, x] = turned * (2.0 / half_range) - vector(j - 1)[x]

    def sketch_row(j):
        turned = (images[j] * sign[...]).reshape(cells, nz)
        high = turned.astype(jnp.bfloat16)
        low = (turned - high.astype(jnp.float32)).astype(jnp.bfloat16)
        both = jnp.concatenate([high, low], axis=0)
        sampled = jnp.dot(both, table[...], preferred_element_type=jnp.float32)
        sampled = (sampled[:cells] + sampled[cells:]) * weights[...].reshape(cells, wide)
        total = jnp.sum(sampled, axis=0, keepdims=True)
        folded = total[:, :LANES]
        for k in range(1, wide // LANES):
            folded = folded + total[:, k * LANES : (k + 1) * LANES]
        spread = folded
        for k in range(1, LANES // share):
            spread = spread + pltpu.roll(folded, k * share, 1)
        rows[pl.ds(j, 1), :] = spread

    @pl.loop(0, ITERS)
    def _(restart):
        for j in range(BASIS):
            stencil_step(j)
            if j in (1, 3, 5):

                @pl.when(restart == 0)
                def _():
                    arrive(2, j // 2)
                    begin(2, j // 2 + 1)

        @pl.when(restart == 0)
        def _():
            arrive(2, 3)

        @pl.loop(0, BASIS + 1, unroll=3)
        def _(j):
            sketch_row(j)

        buffer = sums.at[restart]
        behind = (lane // share == 1) & (lax.broadcasted_iota(jnp.int32, (BASIS, LANES), 0) == 0)
        tile = jnp.where(behind, rows[BASIS : BASIS + 1, :], rows[0:BASIS, :])
        buffer[pl.ds(at["gx"], 1), pl.ds(at["gy"], 1), pl.ds(at["gz"], 1)] = tile.reshape(
            1, 1, 1, BASIS, LANES
        )

        def shares(place, whole):
            rest = [slice(None)] * 2 if whole else [pl.ds(place[axis], 1) for axis in ("gy", "gz")]
            return buffer.at[(pl.ds(place["gx"], 1), *rest)]

        small = restart * peers
        started = []
        for hops, whole in ((plane_hops, False), (line_hops, True)):
            arrivals = []
            for target, origin in hops:
                sems = dict(send_sem=small_send.at[small], recv_sem=small_recv.at[small])
                go = dict(device_id=target, device_id_type=MESH)
                small = small + 1
                source, landing = shares(at, whole), shares({**at, **origin}, whole)
                copy = pltpu.make_async_remote_copy(src_ref=source, dst_ref=source, **sems, **go)
                copy.start()
                started.append(copy)
                arrivals.append(
                    pltpu.make_async_remote_copy(src_ref=landing, dst_ref=landing, **sems, **go)
                )
            for copy in arrivals:
                copy.wait_recv()
        devices = math.prod(sizes.values())
        tiles = buffer[...].reshape(devices, BASIS, LANES)
        sketched = [jnp.where(lane < share, tiles[:, j, :], 0.0) for j in range(BASIS)]
        aside = pltpu.roll(tiles[:, 0, :], LANES - share, 1)
        solved = solve_rows(sketched, jnp.where(lane < share, aside, 0.0))
        for copy in started:
            copy.wait_send()

        total = sol_ref[...]
        for j in range(BASIS):
            total = total + solved[j].reshape(1, 1, 1) * vector(j)[own]
        sol_ref[...] = total

        @pl.when(restart == 0)
        def _():
            for plan in plans:
                for sends, _ in plan:
                    for copy in sends:
                        copy.wait_send()

        @pl.when(restart == ITERS - 1)
        def _():
            left = field[own]
            for j in range(BASIS):
                left = left - solved[j].reshape(1, 1, 1) * images[(j,) + own]
            res_ref[...] = left

        @pl.when(restart < ITERS - 1)
        def _():
            for x in range(nx):
                left = field[x]
                for j in range(BASIS):
                    left = left - solved[j] * images[j, x]
                field[x] = left


def whole_fits(sizes, nx, ny, nz, sampled):
    devices = math.prod(sizes.values())
    share = sampled // devices
    if sizes["gy"] % 2 or sampled % devices or share == 0 or LANES % share or 2 * share > LANES:
        return False
    if nz % LANES or nz // sizes["gz"] != LANES or (ny // sizes["gy"]) % 8 or ny % 16:
        return False
    return nx * ny * nz * 4 * (2 * BASIS + 8) <= 24 * 1024 * 1024


def whole_shards(sizes, right_side, diagonal, sign_bits, freq_x, freq_y, freq_z):
    block = right_side.shape
    nx, ny, nz = (size * sizes[axis] for size, axis in zip(block, ("gx", "gy", "gz")))
    share = freq_x.shape[0] // math.prod(sizes.values())
    wide = -(-3 * share // LANES) * LANES
    freqs = [f.reshape(-1, LANES) for f in (freq_x, freq_y, freq_z)]
    f32 = jnp.float32
    copies = copies_needed(sizes)
    smalls = ITERS * (sizes["gx"] - 1 + sizes["gy"] * sizes["gz"] - 1)
    return pl.pallas_call(
        functools.partial(whole_kernel, sizes, share),
        out_shape=[jax.ShapeDtypeStruct(block, f32)] * 2,
        in_specs=[pl.BlockSpec(memory_space=pltpu.HBM)] * 6,
        out_specs=[pl.BlockSpec(memory_space=pltpu.VMEM)] * 2,
        scratch_shapes=[
            pltpu.VMEM((BASIS + 1, nx, ny, nz), f32),
            pltpu.VMEM((nx, ny, nz), f32),
            pltpu.VMEM((nx, ny, nz), f32),
            pltpu.VMEM((BASIS - 1, nx, ny, nz), f32),
            pltpu.VMEM((nz, wide), jnp.bfloat16),
            pltpu.VMEM((nx, ny, wide), f32),
            pltpu.VMEM((16, LANES), f32),
            pltpu.VMEM((ITERS, sizes["gx"], sizes["gy"], sizes["gz"], BASIS, LANES), f32),
            pltpu.VMEM(block, jnp.int32),
            pltpu.VMEM((3,) + freqs[0].shape, jnp.int32),
            pltpu.SemaphoreType.DMA((6,)),
            pltpu.SemaphoreType.DMA((copies,)),
            pltpu.SemaphoreType.DMA((copies,)),
            pltpu.SemaphoreType.DMA((smalls,)),
            pltpu.SemaphoreType.DMA((smalls,)),
        ],
        compiler_params=pltpu.CompilerParams(
            collective_id=0, has_side_effects=True, vmem_limit_bytes=56 * 1024 * 1024
        ),
    )(right_side, diagonal, sign_bits, *freqs)


def solution(mesh):
    in_specs = (P("gx", "gy", "gz"), P("gx", "gy", "gz"), P("gx", "gy", "gz"), P(), P(), P())
    out_specs = (P("gx", "gy", "gz"), P("gx", "gy", "gz"))
    sizes = {axis: mesh.shape[axis] for axis in ("gx", "gy", "gz")}

    def run(right_side, diagonal, sign_bits, freq_x, freq_y, freq_z):
        plan = shards
        if whole_fits(sizes, *right_side.shape, freq_x.shape[0]):
            plan = functools.partial(whole_shards, sizes)
        mapped = jax.shard_map(
            plan, mesh=mesh, in_specs=in_specs, out_specs=out_specs, check_vma=False
        )
        return mapped(right_side, diagonal, sign_bits, freq_x, freq_y, freq_z)

    return run
```

```python
import functools
import math

import jax
import jax.numpy as jnp
from jax import lax
from jax.experimental import pallas as pl
from jax.experimental.pallas import tpu as pltpu
from jax.sharding import PartitionSpec as P

BASIS = 8
ITERS = 2


center_value = 7.0
half_range = 7.0
tiny_value = 1e-06
highest = lax.Precision.HIGHEST


def extended(shard, sides, width):
    for axis, dim in sides:
        size, length = (lax.axis_size(axis), shard.shape[dim])
        up = [(i, (i + 1) % size) for i in range(size - 1)]
        down = [(j, i) for i, j in up]
        last = lax.slice_in_dim(shard, length - width, length, axis=dim)
        first = lax.slice_in_dim(shard, 0, width, axis=dim)
        before = lax.ppermute(last, axis, up)
        after = lax.ppermute(first, axis, down)
        shard = jnp.concatenate([before, shard, after], axis=dim)
    return shard


def stencil(padded, diagonal):
    beside = padded[2:, 1:-1, 1:-1] + padded[:-2, 1:-1, 1:-1]
    beside = beside + padded[1:-1, 2:, 1:-1] + padded[1:-1, :-2, 1:-1]
    beside = beside + padded[1:-1, 1:-1, 2:] + padded[1:-1, 1:-1, :-2]
    return (6.0 + diagonal) * padded[1:-1, 1:-1, 1:-1] - beside


def cosine_table(freqs, offset, count, length):
    indices = offset + jnp.arange(count, dtype=jnp.int32)
    phases = (2 * indices[:, None] + 1) * freqs[None, :] % (4 * length)
    return (jnp.sqrt(2.0 / length) * jnp.cos(jnp.pi * phases / (2.0 * length))).astype(jnp.float32)


def least_squares(matrix):
    count = matrix.shape[0] - 1
    target = matrix[count]
    orthonormal = []
    upper = {}
    for column_at in range(count):
        column = matrix[column_at]
        for repeat in range(2):
            for earlier in range(column_at):
                amount = jnp.dot(orthonormal[earlier], column, precision=highest)
                column = column - amount * orthonormal[earlier]
                upper[earlier, column_at] = upper.get((earlier, column_at), 0.0) + amount
        length = jnp.sqrt(jnp.dot(column, column, precision=highest) + tiny_value)
        orthonormal.append(column / length)
        upper[column_at, column_at] = length
    projected = [jnp.dot(basis_row, target, precision=highest) for basis_row in orthonormal]
    solved = [None] * count
    for row_at in range(count - 1, -1, -1):
        value = projected[row_at]
        for later in range(row_at + 1, count):
            value = value - upper[row_at, later] * solved[later]
        solved[row_at] = value / upper[row_at, row_at]
    return jnp.stack(solved)


def basis_plain(residual, diagonal):
    vectors = [residual]
    images = []
    for position in range(BASIS):
        padded = extended(vectors[position], (("gx", 0), ("gy", 1), ("gz", 2)), 1)
        image = stencil(padded, diagonal)
        images.append(image)
        if position + 1 < BASIS:
            turned = (image - center_value * vectors[position]) / half_range
            vectors.append(turned if position == 0 else 2.0 * turned - vectors[position - 1])
    return (vectors, images)


def local_sketch(columns, signs, table_x, table_y, table_z):
    flipped = jnp.stack(columns, axis=2) * signs[:, :, None, :]
    size_x, size_y, count, depth = flipped.shape
    rows_flat = flipped.reshape(-1, depth)
    weights = table_x[:, None, :] * table_y[None, :, :]
    sampled = table_z.shape[1]
    block = min(512, sampled)
    pieces = []
    for begin in range(0, sampled, block):
        inner_sums = jnp.dot(
            rows_flat,
            table_z[:, begin : begin + block],
            precision=highest,
            preferred_element_type=jnp.float32,
        )
        inner_sums = inner_sums.reshape(size_x, size_y, count, block)
        pieces.append(
            jnp.einsum(
                "xyjs,xys->js", inner_sums, weights[:, :, begin : begin + block], precision=highest
            )
        )
    return jnp.concatenate(pieces, axis=1)


def shards(right_side, diagonal, sign_bits, freq_x, freq_y, freq_z):
    size_x, size_y, size_z = right_side.shape
    table_x = cosine_table(
        freq_x, lax.axis_index("gx") * size_x, size_x, size_x * lax.axis_size("gx")
    )
    table_y = cosine_table(
        freq_y, lax.axis_index("gy") * size_y, size_y, size_y * lax.axis_size("gy")
    )
    table_z = cosine_table(
        freq_z, lax.axis_index("gz") * size_z, size_z, size_z * lax.axis_size("gz")
    )
    signs = 1.0 - 2.0 * sign_bits.astype(jnp.float32)
    solution = jnp.zeros_like(right_side)
    residual = right_side
    for restart in range(ITERS):
        vectors, images = basis_plain(residual, diagonal)
        partial_value = local_sketch(images + [residual], signs, table_x, table_y, table_z)
        shares = lax.psum_scatter(partial_value, "gx", scatter_dimension=1, tiled=True)
        shares = lax.psum(shares, ("gy", "gz"))
        matrix = lax.all_gather(shares, "gx", axis=1, tiled=True)
        weights_solved = least_squares(matrix)
        for position in range(BASIS):
            solution = solution + weights_solved[position] * vectors[position]
            residual = residual - weights_solved[position] * images[position]
    return (solution, residual)


MESH = pl.DeviceIdType.MESH
LANES = 128
SINE = [(-1.0) ** k / math.factorial(2 * k + 1) for k in range(7)]


def cosines(freqs, count, length):
    cells = lax.broadcasted_iota(jnp.int32, (count, freqs.shape[1]), 0)
    phases = lax.rem((2 * cells + 1) * freqs, 4 * length)
    folded = length - jnp.minimum(phases, 4 * length - phases)
    angle = folded.astype(jnp.float32) * (math.pi / (2.0 * length))
    square = angle * angle
    value = jnp.full_like(angle, SINE[-1])
    for term in SINE[-2::-1]:
        value = value * square + term
    return value * angle * math.sqrt(2.0 / length)


def total_of(value):
    return jnp.sum(jnp.sum(value, axis=0, keepdims=True), axis=1, keepdims=True)


def swept(left, among, short):
    count, left, amounts = len(left), list(left), []
    for e in range(count):
        amount = left[e]
        amounts.append(amount)
        left[e] = amount * short[e]
        for f in range(count):
            if f != e:
                left[f] = left[f] - amount * among[max(e, f)][min(e, f)]
    return amounts, left


def solve_rows(rows, target):
    count = len(rows)
    inner = [[total_of(rows[i] * rows[j]) for j in range(i, count)] for i in range(count)]
    basis, onto, among, short, upper, inverse = [], [], [], [], {}, []
    for at_column in range(count):
        column, square, left = rows[at_column], inner[at_column][0], []
        amounts = [0.0] * at_column
        if at_column:
            first, _ = swept([onto[e][at_column] for e in range(at_column)], among, short)
            for e in range(at_column):
                column = column - first[e] * basis[e]
            start = [total_of(q * column) for q in basis]
            square = total_of(column * column)
            second, left = swept(start, among, short)
            for e in range(at_column):
                column = column - second[e] * basis[e]
                square = square - second[e] * (start[e] + left[e])
                amounts[e] = first[e] + second[e]
                upper[e, at_column] = amounts[e]
        scale = lax.rsqrt(jnp.maximum(square, 0.0) + tiny_value)
        basis.append(column * scale)
        along = {}
        for j in range(at_column + 1, count):
            value = inner[at_column][j - at_column]
            for e in range(at_column):
                value = value - amounts[e] * onto[e][j]
            along[j] = value * scale
        onto.append(along)
        among.append([value * scale for value in left])
        short.append(tiny_value * scale * scale)
        inverse.append(scale)
    projected = [total_of(q * target) for q in basis]
    solved = [None] * count
    for row in range(count - 1, -1, -1):
        value = projected[row]
        for later in range(row + 1, count):
            value = value - upper[row, later] * solved[later]
        solved[row] = value * inverse[row]
    return solved


class Gather:
    def __init__(self, sizes, block, send_sem, recv_sem):
        self.sizes, self.block = sizes, block
        self.send_sem, self.recv_sem = send_sem, recv_sem
        self.count = 0
        self.at = {axis: lax.axis_index(axis) for axis in sizes}

    def regions(self, ref, state, at):
        bx, by, bz = self.block
        gx, gy, gz = at["gx"], at["gy"], at["gz"]
        xs = slice(None) if state["x"] == "all" else pl.ds(gx * bx, bx)
        zs = slice(None) if state["z"] == "all" else pl.ds(pl.multiple_of(gz * bz, bz), bz)
        if state["y"] == "own":
            ys = [gy]
        else:
            ys = [lax.rem(gy, 2) + 2 * k for k in range(self.sizes["gy"] // 2)]
        return [ref.at[xs, pl.ds(pl.multiple_of(y * by, by), by), zs] for y in ys]

    def plan(self, ref, state, phase, held=None):
        axis = {"X": "gx", "Z": "gz", "H": "gy", "C": "gy"}[phase]
        size, here = self.sizes[axis], self.at[axis]
        if phase == "C":
            hops = [(here + 1 - 2 * lax.rem(here, 2), here + 1 - 2 * lax.rem(here, 2))]
        else:
            stride = 2 if phase == "H" else 1
            hops = [
                (lax.rem(here + k, size), lax.rem(here + size - k, size))
                for k in range(stride, size, stride)
            ]
        sends, arriving = [], []
        for target, origin in hops:
            mine = self.regions(ref, state, self.at)
            theirs = self.regions(ref, state, {**self.at, axis: origin})
            for source, landing in zip(mine, theirs):
                n = self.count
                self.count += 1
                sems = dict(send_sem=self.send_sem.at[n], recv_sem=self.recv_sem.at[n])
                go = dict(device_id={axis: target}, device_id_type=MESH)
                sends.append(
                    pltpu.make_async_remote_copy(
                        src_ref=source if held is None else held, dst_ref=source, **sems, **go
                    )
                )
                arriving.append(
                    pltpu.make_async_remote_copy(src_ref=landing, dst_ref=landing, **sems, **go)
                )
        if phase == "X":
            state["x"] = "all"
        elif phase == "Z":
            state["z"] = "all"
        elif phase == "H":
            state["y"] = "half"
        else:
            state["y"] = "all"
        return sends, arriving


def copies_needed(sizes):
    half = sizes["gy"] // 2
    return 3 * (sizes["gx"] - 1 + (sizes["gz"] - 1) * half + half - 1 + half) + 8


def whole_kernel(
    sizes, share, right_ref, diagonal_ref, bits_ref, fx_ref, fy_ref, fz_ref, sol_ref, res_ref,
    images, diag, sign, vectors, table, weights, rows, sums, bits, freqs, load_sem, send_sem,
    recv_sem, small_send, small_recv,
):
    bx, by, bz = right_ref.shape
    _, nx, ny, nz = images.shape
    wide = table.shape[1]
    cells = nx * ny
    at = {axis: lax.axis_index(axis) for axis in sizes}
    x0 = at["gx"] * bx
    y0 = pl.multiple_of(at["gy"] * by, by)
    z0 = pl.multiple_of(at["gz"] * bz, bz)
    own = (pl.ds(x0, bx), pl.ds(y0, by), pl.ds(z0, bz))
    field = images.at[BASIS]

    loads = [
        pltpu.make_async_copy(source, target, load_sem.at[n])
        for n, (source, target) in enumerate(
            [
                (right_ref, field.at[own]),
                (diagonal_ref, diag.at[own]),
                (bits_ref, bits),
                (fx_ref, freqs.at[0]),
                (fy_ref, freqs.at[1]),
                (fz_ref, freqs.at[2]),
            ]
        )
    ]
    for copy in loads:
        copy.start()
    barrier = pltpu.get_barrier_semaphore()
    side = sizes["gy"] * sizes["gz"]
    across = at["gy"] * sizes["gz"] + at["gz"]

    def member(index):
        return {"gy": lax.div(index, sizes["gz"]), "gz": lax.rem(index, sizes["gz"])}

    plane_hops = [
        (member(lax.rem(across + k, side)), member(lax.rem(across + side - k, side)))
        for k in range(1, side)
    ]
    line_hops = [
        (
            {"gx": lax.rem(at["gx"] + k, sizes["gx"])},
            {"gx": lax.rem(at["gx"] + sizes["gx"] - k, sizes["gx"])},
        )
        for k in range(1, sizes["gx"])
    ]
    for target, _ in plane_hops + line_hops:
        pl.semaphore_signal(barrier, inc=1, device_id=target, device_id_type=MESH)
    peers = len(plane_hops + line_hops)

    gather = Gather(sizes, (bx, by, bz), send_sem, recv_sem)
    plans = []
    for ref, order, held in [
        (field, "XZHC", right_ref),
        (diag, "XHZC", diagonal_ref),
        (sign, "XZHC", None),
    ]:
        state = {"x": "own", "y": "own", "z": "own"}
        plans.append(
            [gather.plan(ref, state, phase, held if phase == "X" else None) for phase in order]
        )

    def begin(array, step):
        for copy in plans[array][step][0]:
            copy.start()

    def arrive(array, step):
        for copy in plans[array][step][1]:
            copy.wait_recv()

    pl.semaphore_wait(barrier, peers)
    begin(0, 0)
    begin(1, 0)
    for copy in loads:
        copy.wait()
    sol_ref[...] = jnp.zeros_like(sol_ref)
    sign[own] = 1.0 - 2.0 * bits[...].astype(jnp.float32)
    begin(2, 0)

    me = (at["gx"] * sizes["gy"] + at["gy"]) * sizes["gz"] + at["gz"]
    lane = lax.broadcasted_iota(jnp.int32, (1, LANES), 1)

    def own_rows(number):
        begin_at = me * share
        row = freqs[number, pl.ds(begin_at // LANES, 1), :]
        part = lax.rem(begin_at, LANES) // share
        spread = row
        for k in range(LANES // share):
            turned = row
            for group in range(LANES // share):
                shift = ((group - k) * share) % LANES
                moved = pltpu.roll(row, shift, 1) if shift else row
                turned = jnp.where(lane // share == group, moved, turned)
            spread = jnp.where(part == k, turned, spread)
        return jnp.concatenate([spread] * (wide // LANES), axis=1)

    def tables():
        cos_x = cosines(own_rows(0), nx, nx)
        cos_y = cosines(own_rows(1), ny, ny)
        for x in range(nx):
            weights[x] = cos_x[x : x + 1] * cos_y
        group = lax.broadcasted_iota(jnp.int32, (nz, wide), 1) // share
        cos_z = cosines(own_rows(2), nz, nz)
        first = cos_z.astype(jnp.bfloat16).astype(jnp.float32)
        second = (cos_z - first).astype(jnp.bfloat16).astype(jnp.float32)
        third = cos_z - first - second
        chosen = jnp.where(group == 0, first, jnp.where(group == 1, second, third))
        held = jnp.where(group < 3, chosen, 0.0).astype(jnp.bfloat16)
        table[0:nz] = held
        table[nz : 2 * nz] = held

    for step in range(1, 4):
        for array in range(2):
            arrive(array, step - 1)
            begin(array, step)
        if step == 1:
            tables()
    arrive(0, 3)
    arrive(1, 3)

    def beside_along_y(plane):
        tiles = plane.reshape(ny // 8, 8, nz)
        row_at = lax.broadcasted_iota(jnp.int32, tiles.shape, 1)
        outside = jnp.zeros((1, 8, nz), jnp.float32)
        down, up = pltpu.roll(tiles, 1, 1), pltpu.roll(tiles, 7, 1)
        below = jnp.where(row_at == 0, jnp.concatenate([outside, down[:-1]], axis=0), down)
        above = jnp.where(row_at == 7, jnp.concatenate([up[1:], outside], axis=0), up)
        return (below + above).reshape(ny, nz)

    def beside_along_z(plane):
        parts = nz // LANES
        lane_at = lax.broadcasted_iota(jnp.int32, (ny, LANES), 1)
        cut = [plane[:, c * LANES : (c + 1) * LANES] for c in range(parts)]
        later = [pltpu.roll(part, 1, 1) for part in cut]
        sooner = [pltpu.roll(part, LANES - 1, 1) for part in cut]
        summed = []
        for c in range(parts):
            low = later[c - 1] if c else 0.0
            high = sooner[c + 1] if c + 1 < parts else 0.0
            summed.append(
                jnp.where(lane_at == 0, low, later[c])
                + jnp.where(lane_at == LANES - 1, high, sooner[c])
            )
        return jnp.concatenate(summed, axis=1)

    def vector(j):
        return field if j == 0 else vectors.at[j - 1]

    def stencil_step(j):
        here_ref = vector(j)
        for x in range(nx):
            here = here_ref[x]
            beside = None
            for near in (x + 1, x - 1):
                if 0 <= near < nx:
                    beside = here_ref[near] if beside is None else beside + here_ref[near]
            beside = beside + beside_along_y(here) + beside_along_z(here)
            image = (6.0 + diag[x]) * here - beside
            images[j, x] = image
            if j + 1 < BASIS:
                turned = image - center_value * here
                if j == 0:
                    vectors[j, x] = turned * (1.0 / half_range)
                else:
                    vectors[j, x] = turned * (2.0 / half_range) - vector(j - 1)[x]

    def sketch_row(j):
        turned = (images[j] * sign[...]).reshape(cells, nz)
        high = turned.astype(jnp.bfloat16)
        low = (turned - high.astype(jnp.float32)).astype(jnp.bfloat16)
        both = jnp.concatenate([high, low], axis=1)
        sampled = jnp.dot(both, table[...], preferred_element_type=jnp.float32)
        sampled = sampled * weights[...].reshape(cells, wide)
        total = jnp.sum(sampled, axis=0, keepdims=True)
        folded = total[:, :LANES]
        for k in range(1, wide // LANES):
            folded = folded + total[:, k * LANES : (k + 1) * LANES]
        spread = folded
        for k in range(1, LANES // share):
            spread = spread + pltpu.roll(folded, k * share, 1)
        rows[pl.ds(j, 1), :] = spread

    @pl.loop(0, ITERS)
    def _(restart):
        for j in range(BASIS):
            stencil_step(j)
            if j in (1, 3, 5):

                @pl.when(restart == 0)
                def _():
                    arrive(2, j // 2)
                    begin(2, j // 2 + 1)

        @pl.when(restart == 0)
        def _():
            arrive(2, 3)

        @pl.loop(0, BASIS + 1, unroll=3)
        def _(j):
            sketch_row(j)

        buffer = sums.at[restart]
        behind = (lane // share == 1) & (lax.broadcasted_iota(jnp.int32, (BASIS, LANES), 0) == 0)
        tile = jnp.where(behind, rows[BASIS : BASIS + 1, :], rows[0:BASIS, :])
        buffer[pl.ds(at["gx"], 1), pl.ds(at["gy"], 1), pl.ds(at["gz"], 1)] = tile.reshape(
            1, 1, 1, BASIS, LANES
        )

        def shares(place, whole):
            rest = [slice(None)] * 2 if whole else [pl.ds(place[axis], 1) for axis in ("gy", "gz")]
            return buffer.at[(pl.ds(place["gx"], 1), *rest)]

        small = restart * peers
        started = []
        for hops, whole in ((plane_hops, False), (line_hops, True)):
            arrivals = []
            for target, origin in hops:
                sems = dict(send_sem=small_send.at[small], recv_sem=small_recv.at[small])
                go = dict(device_id=target, device_id_type=MESH)
                small = small + 1
                source, landing = shares(at, whole), shares({**at, **origin}, whole)
                copy = pltpu.make_async_remote_copy(src_ref=source, dst_ref=source, **sems, **go)
                copy.start()
                started.append(copy)
                arrivals.append(
                    pltpu.make_async_remote_copy(src_ref=landing, dst_ref=landing, **sems, **go)
                )
            for copy in arrivals:
                copy.wait_recv()
        devices = math.prod(sizes.values())
        tiles = buffer[...].reshape(devices, BASIS, LANES)
        sketched = [jnp.where(lane < share, tiles[:, j, :], 0.0) for j in range(BASIS)]
        aside = pltpu.roll(tiles[:, 0, :], LANES - share, 1)
        solved = solve_rows(sketched, jnp.where(lane < share, aside, 0.0))
        for copy in started:
            copy.wait_send()

        total = sol_ref[...]
        for j in range(BASIS):
            total = total + solved[j].reshape(1, 1, 1) * vector(j)[own]
        sol_ref[...] = total

        @pl.when(restart == 0)
        def _():
            for plan in plans:
                for sends, _ in plan:
                    for copy in sends:
                        copy.wait_send()

        @pl.when(restart == ITERS - 1)
        def _():
            left = field[own]
            for j in range(BASIS):
                left = left - solved[j].reshape(1, 1, 1) * images[(j,) + own]
            res_ref[...] = left

        @pl.when(restart < ITERS - 1)
        def _():
            for x in range(nx):
                left = field[x]
                for j in range(BASIS):
                    left = left - solved[j] * images[j, x]
                field[x] = left


def whole_fits(sizes, nx, ny, nz, sampled):
    devices = math.prod(sizes.values())
    share = sampled // devices
    if sizes["gy"] % 2 or sampled % devices or share == 0 or LANES % share or 2 * share > LANES:
        return False
    if nz % LANES or nz // sizes["gz"] != LANES or (ny // sizes["gy"]) % 8 or ny % 16:
        return False
    return nx * ny * nz * 4 * (2 * BASIS + 8) <= 24 * 1024 * 1024


def whole_shards(sizes, right_side, diagonal, sign_bits, freq_x, freq_y, freq_z):
    block = right_side.shape
    nx, ny, nz = (size * sizes[axis] for size, axis in zip(block, ("gx", "gy", "gz")))
    share = freq_x.shape[0] // math.prod(sizes.values())
    wide = -(-3 * share // LANES) * LANES
    freqs = [f.reshape(-1, LANES) for f in (freq_x, freq_y, freq_z)]
    f32 = jnp.float32
    copies = copies_needed(sizes)
    smalls = ITERS * (sizes["gx"] - 1 + sizes["gy"] * sizes["gz"] - 1)
    return pl.pallas_call(
        functools.partial(whole_kernel, sizes, share),
        out_shape=[jax.ShapeDtypeStruct(block, f32)] * 2,
        in_specs=[pl.BlockSpec(memory_space=pltpu.HBM)] * 6,
        out_specs=[pl.BlockSpec(memory_space=pltpu.VMEM)] * 2,
        scratch_shapes=[
            pltpu.VMEM((BASIS + 1, nx, ny, nz), f32),
            pltpu.VMEM((nx, ny, nz), f32),
            pltpu.VMEM((nx, ny, nz), f32),
            pltpu.VMEM((BASIS - 1, nx, ny, nz), f32),
            pltpu.VMEM((2 * nz, wide), jnp.bfloat16),
            pltpu.VMEM((nx, ny, wide), f32),
            pltpu.VMEM((16, LANES), f32),
            pltpu.VMEM((ITERS, sizes["gx"], sizes["gy"], sizes["gz"], BASIS, LANES), f32),
            pltpu.VMEM(block, jnp.int32),
            pltpu.VMEM((3,) + freqs[0].shape, jnp.int32),
            pltpu.SemaphoreType.DMA((6,)),
            pltpu.SemaphoreType.DMA((copies,)),
            pltpu.SemaphoreType.DMA((copies,)),
            pltpu.SemaphoreType.DMA((smalls,)),
            pltpu.SemaphoreType.DMA((smalls,)),
        ],
        compiler_params=pltpu.CompilerParams(
            collective_id=0, has_side_effects=True, vmem_limit_bytes=56 * 1024 * 1024
        ),
    )(right_side, diagonal, sign_bits, *freqs)


def solution(mesh):
    in_specs = (P("gx", "gy", "gz"), P("gx", "gy", "gz"), P("gx", "gy", "gz"), P(), P(), P())
    out_specs = (P("gx", "gy", "gz"), P("gx", "gy", "gz"))
    sizes = {axis: mesh.shape[axis] for axis in ("gx", "gy", "gz")}

    def run(right_side, diagonal, sign_bits, freq_x, freq_y, freq_z):
        plan = shards
        if whole_fits(sizes, *right_side.shape, freq_x.shape[0]):
            plan = functools.partial(whole_shards, sizes)
        mapped = jax.shard_map(
            plan, mesh=mesh, in_specs=in_specs, out_specs=out_specs, check_vma=False
        )
        return mapped(right_side, diagonal, sign_bits, freq_x, freq_y, freq_z)

    return run
```

```python
import functools
import math

import jax
import jax.numpy as jnp
from jax import lax
from jax.experimental import pallas as pl
from jax.experimental.pallas import tpu as pltpu
from jax.sharding import PartitionSpec as P

BASIS = 8
ITERS = 2


center_value = 7.0
half_range = 7.0
tiny_value = 1e-06
highest = lax.Precision.HIGHEST


def extended(shard, sides, width):
    for axis, dim in sides:
        size, length = (lax.axis_size(axis), shard.shape[dim])
        up = [(i, (i + 1) % size) for i in range(size - 1)]
        down = [(j, i) for i, j in up]
        last = lax.slice_in_dim(shard, length - width, length, axis=dim)
        first = lax.slice_in_dim(shard, 0, width, axis=dim)
        before = lax.ppermute(last, axis, up)
        after = lax.ppermute(first, axis, down)
        shard = jnp.concatenate([before, shard, after], axis=dim)
    return shard


def stencil(padded, diagonal):
    beside = padded[2:, 1:-1, 1:-1] + padded[:-2, 1:-1, 1:-1]
    beside = beside + padded[1:-1, 2:, 1:-1] + padded[1:-1, :-2, 1:-1]
    beside = beside + padded[1:-1, 1:-1, 2:] + padded[1:-1, 1:-1, :-2]
    return (6.0 + diagonal) * padded[1:-1, 1:-1, 1:-1] - beside


def cosine_table(freqs, offset, count, length):
    indices = offset + jnp.arange(count, dtype=jnp.int32)
    phases = (2 * indices[:, None] + 1) * freqs[None, :] % (4 * length)
    return (jnp.sqrt(2.0 / length) * jnp.cos(jnp.pi * phases / (2.0 * length))).astype(jnp.float32)


def least_squares(matrix):
    count = matrix.shape[0] - 1
    target = matrix[count]
    orthonormal = []
    upper = {}
    for column_at in range(count):
        column = matrix[column_at]
        for repeat in range(2):
            for earlier in range(column_at):
                amount = jnp.dot(orthonormal[earlier], column, precision=highest)
                column = column - amount * orthonormal[earlier]
                upper[earlier, column_at] = upper.get((earlier, column_at), 0.0) + amount
        length = jnp.sqrt(jnp.dot(column, column, precision=highest) + tiny_value)
        orthonormal.append(column / length)
        upper[column_at, column_at] = length
    projected = [jnp.dot(basis_row, target, precision=highest) for basis_row in orthonormal]
    solved = [None] * count
    for row_at in range(count - 1, -1, -1):
        value = projected[row_at]
        for later in range(row_at + 1, count):
            value = value - upper[row_at, later] * solved[later]
        solved[row_at] = value / upper[row_at, row_at]
    return jnp.stack(solved)


def basis_plain(residual, diagonal):
    vectors = [residual]
    images = []
    for position in range(BASIS):
        padded = extended(vectors[position], (("gx", 0), ("gy", 1), ("gz", 2)), 1)
        image = stencil(padded, diagonal)
        images.append(image)
        if position + 1 < BASIS:
            turned = (image - center_value * vectors[position]) / half_range
            vectors.append(turned if position == 0 else 2.0 * turned - vectors[position - 1])
    return (vectors, images)


def local_sketch(columns, signs, table_x, table_y, table_z):
    flipped = jnp.stack(columns, axis=2) * signs[:, :, None, :]
    size_x, size_y, count, depth = flipped.shape
    rows_flat = flipped.reshape(-1, depth)
    weights = table_x[:, None, :] * table_y[None, :, :]
    sampled = table_z.shape[1]
    block = min(512, sampled)
    pieces = []
    for begin in range(0, sampled, block):
        inner_sums = jnp.dot(
            rows_flat,
            table_z[:, begin : begin + block],
            precision=highest,
            preferred_element_type=jnp.float32,
        )
        inner_sums = inner_sums.reshape(size_x, size_y, count, block)
        pieces.append(
            jnp.einsum(
                "xyjs,xys->js", inner_sums, weights[:, :, begin : begin + block], precision=highest
            )
        )
    return jnp.concatenate(pieces, axis=1)


def shards(right_side, diagonal, sign_bits, freq_x, freq_y, freq_z):
    size_x, size_y, size_z = right_side.shape
    table_x = cosine_table(
        freq_x, lax.axis_index("gx") * size_x, size_x, size_x * lax.axis_size("gx")
    )
    table_y = cosine_table(
        freq_y, lax.axis_index("gy") * size_y, size_y, size_y * lax.axis_size("gy")
    )
    table_z = cosine_table(
        freq_z, lax.axis_index("gz") * size_z, size_z, size_z * lax.axis_size("gz")
    )
    signs = 1.0 - 2.0 * sign_bits.astype(jnp.float32)
    solution = jnp.zeros_like(right_side)
    residual = right_side
    for restart in range(ITERS):
        vectors, images = basis_plain(residual, diagonal)
        partial_value = local_sketch(images + [residual], signs, table_x, table_y, table_z)
        shares = lax.psum_scatter(partial_value, "gx", scatter_dimension=1, tiled=True)
        shares = lax.psum(shares, ("gy", "gz"))
        matrix = lax.all_gather(shares, "gx", axis=1, tiled=True)
        weights_solved = least_squares(matrix)
        for position in range(BASIS):
            solution = solution + weights_solved[position] * vectors[position]
            residual = residual - weights_solved[position] * images[position]
    return (solution, residual)


MESH = pl.DeviceIdType.MESH
LANES = 128
SINE = [(-1.0) ** k / math.factorial(2 * k + 1) for k in range(7)]


def cosines(freqs, count, length):
    cells = lax.broadcasted_iota(jnp.int32, (count, freqs.shape[1]), 0)
    phases = lax.rem((2 * cells + 1) * freqs, 4 * length)
    folded = length - jnp.minimum(phases, 4 * length - phases)
    angle = folded.astype(jnp.float32) * (math.pi / (2.0 * length))
    square = angle * angle
    value = jnp.full_like(angle, SINE[-1])
    for term in SINE[-2::-1]:
        value = value * square + term
    return value * angle * math.sqrt(2.0 / length)


def total_of(value):
    return jnp.sum(jnp.sum(value, axis=0, keepdims=True), axis=1, keepdims=True)


def swept(left, among, short):
    count, left, amounts = len(left), list(left), []
    for e in range(count):
        amount = left[e]
        amounts.append(amount)
        left[e] = amount * short[e]
        for f in range(count):
            if f != e:
                left[f] = left[f] - amount * among[max(e, f)][min(e, f)]
    return amounts, left


def solve_rows(rows, target):
    count = len(rows)
    inner = [[total_of(rows[i] * rows[j]) for j in range(i, count)] for i in range(count)]
    basis, onto, among, short, upper, inverse = [], [], [], [], {}, []
    for at_column in range(count):
        column, square, left = rows[at_column], inner[at_column][0], []
        amounts = [0.0] * at_column
        if at_column:
            first, _ = swept([onto[e][at_column] for e in range(at_column)], among, short)
            for e in range(at_column):
                column = column - first[e] * basis[e]
            start = [total_of(q * column) for q in basis]
            square = total_of(column * column)
            second, left = swept(start, among, short)
            for e in range(at_column):
                column = column - second[e] * basis[e]
                square = square - second[e] * (start[e] + left[e])
                amounts[e] = first[e] + second[e]
                upper[e, at_column] = amounts[e]
        scale = lax.rsqrt(jnp.maximum(square, 0.0) + tiny_value)
        basis.append(column * scale)
        along = {}
        for j in range(at_column + 1, count):
            value = inner[at_column][j - at_column]
            for e in range(at_column):
                value = value - amounts[e] * onto[e][j]
            along[j] = value * scale
        onto.append(along)
        among.append([value * scale for value in left])
        short.append(tiny_value * scale * scale)
        inverse.append(scale)
    projected = [total_of(q * target) for q in basis]
    solved = [None] * count
    for row in range(count - 1, -1, -1):
        value = projected[row]
        for later in range(row + 1, count):
            value = value - upper[row, later] * solved[later]
        solved[row] = value * inverse[row]
    return solved


class Gather:
    def __init__(self, sizes, block, send_sem, recv_sem):
        self.sizes, self.block = sizes, block
        self.send_sem, self.recv_sem = send_sem, recv_sem
        self.count = 0
        self.at = {axis: lax.axis_index(axis) for axis in sizes}

    def regions(self, ref, state, at):
        bx, by, bz = self.block
        gx, gy, gz = at["gx"], at["gy"], at["gz"]
        xs = slice(None) if state["x"] == "all" else pl.ds(gx * bx, bx)
        zs = slice(None) if state["z"] == "all" else pl.ds(pl.multiple_of(gz * bz, bz), bz)
        if state["y"] == "own":
            ys = [gy]
        else:
            ys = [lax.rem(gy, 2) + 2 * k for k in range(self.sizes["gy"] // 2)]
        return [ref.at[xs, pl.ds(pl.multiple_of(y * by, by), by), zs] for y in ys]

    def plan(self, ref, state, phase, held=None):
        axis = {"X": "gx", "Z": "gz", "H": "gy", "C": "gy"}[phase]
        size, here = self.sizes[axis], self.at[axis]
        if phase == "C":
            hops = [(here + 1 - 2 * lax.rem(here, 2), here + 1 - 2 * lax.rem(here, 2))]
        else:
            stride = 2 if phase == "H" else 1
            hops = [
                (lax.rem(here + k, size), lax.rem(here + size - k, size))
                for k in range(stride, size, stride)
            ]
        sends, arriving = [], []
        for target, origin in hops:
            mine = self.regions(ref, state, self.at)
            theirs = self.regions(ref, state, {**self.at, axis: origin})
            for source, landing in zip(mine, theirs):
                n = self.count
                self.count += 1
                sems = dict(send_sem=self.send_sem.at[n], recv_sem=self.recv_sem.at[n])
                go = dict(device_id={axis: target}, device_id_type=MESH)
                sends.append(
                    pltpu.make_async_remote_copy(
                        src_ref=source if held is None else held, dst_ref=source, **sems, **go
                    )
                )
                arriving.append(
                    pltpu.make_async_remote_copy(src_ref=landing, dst_ref=landing, **sems, **go)
                )
        if phase == "X":
            state["x"] = "all"
        elif phase == "Z":
            state["z"] = "all"
        elif phase == "H":
            state["y"] = "half"
        else:
            state["y"] = "all"
        return sends, arriving


def copies_needed(sizes):
    half = sizes["gy"] // 2
    return 3 * (sizes["gx"] - 1 + (sizes["gz"] - 1) * half + half - 1 + half) + 8


def whole_kernel(
    sizes, share, right_ref, diagonal_ref, bits_ref, fx_ref, fy_ref, fz_ref, sol_ref, res_ref,
    images, diag, sign, even, odd, kept, table, weights, rows, sums, bits, freqs, load_sem, send_sem,
    recv_sem, small_send, small_recv,
):
    bx, by, bz = right_ref.shape
    _, nx, ny, nz = images.shape
    wide = table.shape[1]
    cells = nx * ny
    at = {axis: lax.axis_index(axis) for axis in sizes}
    x0 = at["gx"] * bx
    y0 = pl.multiple_of(at["gy"] * by, by)
    z0 = pl.multiple_of(at["gz"] * bz, bz)
    own = (pl.ds(x0, bx), pl.ds(y0, by), pl.ds(z0, bz))
    field = images.at[BASIS]

    loads = [
        pltpu.make_async_copy(source, target, load_sem.at[n])
        for n, (source, target) in enumerate(
            [
                (right_ref, field.at[own]),
                (diagonal_ref, diag.at[own]),
                (bits_ref, bits),
                (fx_ref, freqs.at[0]),
                (fy_ref, freqs.at[1]),
                (fz_ref, freqs.at[2]),
            ]
        )
    ]
    for copy in loads:
        copy.start()
    barrier = pltpu.get_barrier_semaphore()
    side = sizes["gy"] * sizes["gz"]
    across = at["gy"] * sizes["gz"] + at["gz"]

    def member(index):
        return {"gy": lax.div(index, sizes["gz"]), "gz": lax.rem(index, sizes["gz"])}

    plane_hops = [
        (member(lax.rem(across + k, side)), member(lax.rem(across + side - k, side)))
        for k in range(1, side)
    ]
    line_hops = [
        (
            {"gx": lax.rem(at["gx"] + k, sizes["gx"])},
            {"gx": lax.rem(at["gx"] + sizes["gx"] - k, sizes["gx"])},
        )
        for k in range(1, sizes["gx"])
    ]
    for target, _ in plane_hops + line_hops:
        pl.semaphore_signal(barrier, inc=1, device_id=target, device_id_type=MESH)
    peers = len(plane_hops + line_hops)

    gather = Gather(sizes, (bx, by, bz), send_sem, recv_sem)
    plans = []
    for ref, order, held in [
        (field, "XZHC", right_ref),
        (diag, "XHZC", diagonal_ref),
        (sign, "XZHC", None),
    ]:
        state = {"x": "own", "y": "own", "z": "own"}
        plans.append(
            [gather.plan(ref, state, phase, held if phase == "X" else None) for phase in order]
        )

    def begin(array, step):
        for copy in plans[array][step][0]:
            copy.start()

    def arrive(array, step):
        for copy in plans[array][step][1]:
            copy.wait_recv()

    pl.semaphore_wait(barrier, peers)
    begin(0, 0)
    begin(1, 0)
    for copy in loads:
        copy.wait()
    sol_ref[...] = jnp.zeros_like(sol_ref)
    sign[own] = 1.0 - 2.0 * bits[...].astype(jnp.float32)
    begin(2, 0)

    me = (at["gx"] * sizes["gy"] + at["gy"]) * sizes["gz"] + at["gz"]
    lane = lax.broadcasted_iota(jnp.int32, (1, LANES), 1)

    def own_rows(number):
        begin_at = me * share
        row = freqs[number, pl.ds(begin_at // LANES, 1), :]
        part = lax.rem(begin_at, LANES) // share
        spread = row
        for k in range(LANES // share):
            turned = row
            for group in range(LANES // share):
                shift = ((group - k) * share) % LANES
                moved = pltpu.roll(row, shift, 1) if shift else row
                turned = jnp.where(lane // share == group, moved, turned)
            spread = jnp.where(part == k, turned, spread)
        return jnp.concatenate([spread] * (wide // LANES), axis=1)

    def tables():
        cos_x = cosines(own_rows(0), nx, nx)
        cos_y = cosines(own_rows(1), ny, ny)
        for x in range(nx):
            weights[x] = cos_x[x : x + 1] * cos_y
        group = lax.broadcasted_iota(jnp.int32, (nz, wide), 1) // share
        cos_z = cosines(own_rows(2), nz, nz)
        first = cos_z.astype(jnp.bfloat16).astype(jnp.float32)
        second = (cos_z - first).astype(jnp.bfloat16).astype(jnp.float32)
        third = cos_z - first - second
        chosen = jnp.where(group == 0, first, jnp.where(group == 1, second, third))
        held = jnp.where(group < 3, chosen, 0.0).astype(jnp.bfloat16)
        table[0:nz] = held
        table[nz : 2 * nz] = held

    for step in range(1, 4):
        for array in range(2):
            arrive(array, step - 1)
            begin(array, step)
        if step == 1:
            tables()
    arrive(0, 3)
    arrive(1, 3)

    def beside_along_y(plane):
        tiles = plane.reshape(ny // 8, 8, nz)
        row_at = lax.broadcasted_iota(jnp.int32, tiles.shape, 1)
        outside = jnp.zeros((1, 8, nz), jnp.float32)
        down, up = pltpu.roll(tiles, 1, 1), pltpu.roll(tiles, 7, 1)
        below = jnp.where(row_at == 0, jnp.concatenate([outside, down[:-1]], axis=0), down)
        above = jnp.where(row_at == 7, jnp.concatenate([up[1:], outside], axis=0), up)
        return (below + above).reshape(ny, nz)

    def beside_along_z(plane):
        parts = nz // LANES
        lane_at = lax.broadcasted_iota(jnp.int32, (ny, LANES), 1)
        cut = [plane[:, c * LANES : (c + 1) * LANES] for c in range(parts)]
        later = [pltpu.roll(part, 1, 1) for part in cut]
        sooner = [pltpu.roll(part, LANES - 1, 1) for part in cut]
        summed = []
        for c in range(parts):
            low = later[c - 1] if c else 0.0
            high = sooner[c + 1] if c + 1 < parts else 0.0
            summed.append(
                jnp.where(lane_at == 0, low, later[c])
                + jnp.where(lane_at == LANES - 1, high, sooner[c])
            )
        return jnp.concatenate(summed, axis=1)

    def stencil_step(j, here_ref, other_ref):
        factor = jnp.where(j == 0, 1.0 / half_range, 2.0 / half_range).astype(jnp.float32)
        kept[j] = here_ref[own]
        for x in range(nx):
            here = here_ref[x]
            beside = None
            for near in (x + 1, x - 1):
                if 0 <= near < nx:
                    beside = here_ref[near] if beside is None else beside + here_ref[near]
            beside = beside + beside_along_y(here) + beside_along_z(here)
            image = (6.0 + diag[x]) * here - beside
            images[j, x] = image
            other_ref[x] = (image - center_value * here) * factor - other_ref[x]

    def sketch_row(j):
        turned = (images[j] * sign[...]).reshape(cells, nz)
        high = turned.astype(jnp.bfloat16)
        low = (turned - high.astype(jnp.float32)).astype(jnp.bfloat16)
        both = jnp.concatenate([high, low], axis=1)
        sampled = jnp.dot(both, table[...], preferred_element_type=jnp.float32)
        sampled = sampled * weights[...].reshape(cells, wide)
        total = jnp.sum(sampled, axis=0, keepdims=True)
        folded = total[:, :LANES]
        for k in range(1, wide // LANES):
            folded = folded + total[:, k * LANES : (k + 1) * LANES]
        spread = folded
        for k in range(1, LANES // share):
            spread = spread + pltpu.roll(folded, k * share, 1)
        rows[pl.ds(j, 1), :] = spread

    @pl.loop(0, ITERS)
    def _(restart):
        for x in range(nx):
            even[x] = field[x]
            odd[x] = jnp.zeros((ny, nz), jnp.float32)

        @pl.loop(0, BASIS // 2)
        def _(pair):
            stencil_step(2 * pair, even, odd)
            stencil_step(2 * pair + 1, odd, even)
            for step in range(3):

                @pl.when((restart == 0) & (pair == step))
                def _():
                    arrive(2, step)
                    begin(2, step + 1)

        @pl.when(restart == 0)
        def _():
            arrive(2, 3)

        @pl.loop(0, BASIS + 1, unroll=3)
        def _(j):
            sketch_row(j)

        buffer = sums.at[restart]
        behind = (lane // share == 1) & (lax.broadcasted_iota(jnp.int32, (BASIS, LANES), 0) == 0)
        tile = jnp.where(behind, rows[BASIS : BASIS + 1, :], rows[0:BASIS, :])
        buffer[pl.ds(at["gx"], 1), pl.ds(at["gy"], 1), pl.ds(at["gz"], 1)] = tile.reshape(
            1, 1, 1, BASIS, LANES
        )

        def shares(place, whole):
            rest = [slice(None)] * 2 if whole else [pl.ds(place[axis], 1) for axis in ("gy", "gz")]
            return buffer.at[(pl.ds(place["gx"], 1), *rest)]

        small = restart * peers
        started = []
        for hops, whole in ((plane_hops, False), (line_hops, True)):
            arrivals = []
            for target, origin in hops:
                sems = dict(send_sem=small_send.at[small], recv_sem=small_recv.at[small])
                go = dict(device_id=target, device_id_type=MESH)
                small = small + 1
                source, landing = shares(at, whole), shares({**at, **origin}, whole)
                copy = pltpu.make_async_remote_copy(src_ref=source, dst_ref=source, **sems, **go)
                copy.start()
                started.append(copy)
                arrivals.append(
                    pltpu.make_async_remote_copy(src_ref=landing, dst_ref=landing, **sems, **go)
                )
            for copy in arrivals:
                copy.wait_recv()
        devices = math.prod(sizes.values())
        tiles = buffer[...].reshape(devices, BASIS, LANES)
        sketched = [jnp.where(lane < share, tiles[:, j, :], 0.0) for j in range(BASIS)]
        aside = pltpu.roll(tiles[:, 0, :], LANES - share, 1)
        solved = solve_rows(sketched, jnp.where(lane < share, aside, 0.0))
        for copy in started:
            copy.wait_send()

        total = sol_ref[...]
        for j in range(BASIS):
            total = total + solved[j].reshape(1, 1, 1) * kept[j]
        sol_ref[...] = total

        @pl.when(restart == 0)
        def _():
            for plan in plans:
                for sends, _ in plan:
                    for copy in sends:
                        copy.wait_send()

        @pl.when(restart == ITERS - 1)
        def _():
            left = field[own]
            for j in range(BASIS):
                left = left - solved[j].reshape(1, 1, 1) * images[(j,) + own]
            res_ref[...] = left

        @pl.when(restart < ITERS - 1)
        def _():
            for x in range(nx):
                left = field[x]
                for j in range(BASIS):
                    left = left - solved[j] * images[j, x]
                field[x] = left


def whole_fits(sizes, nx, ny, nz, sampled):
    devices = math.prod(sizes.values())
    share = sampled // devices
    if sizes["gy"] % 2 or sampled % devices or share == 0 or LANES % share or 2 * share > LANES:
        return False
    if nz % LANES or nz // sizes["gz"] != LANES or (ny // sizes["gy"]) % 8 or ny % 16:
        return False
    return nx * ny * nz * 4 * (2 * BASIS + 8) <= 24 * 1024 * 1024


def whole_shards(sizes, right_side, diagonal, sign_bits, freq_x, freq_y, freq_z):
    block = right_side.shape
    nx, ny, nz = (size * sizes[axis] for size, axis in zip(block, ("gx", "gy", "gz")))
    share = freq_x.shape[0] // math.prod(sizes.values())
    wide = -(-3 * share // LANES) * LANES
    freqs = [f.reshape(-1, LANES) for f in (freq_x, freq_y, freq_z)]
    f32 = jnp.float32
    copies = copies_needed(sizes)
    smalls = ITERS * (sizes["gx"] - 1 + sizes["gy"] * sizes["gz"] - 1)
    return pl.pallas_call(
        functools.partial(whole_kernel, sizes, share),
        out_shape=[jax.ShapeDtypeStruct(block, f32)] * 2,
        in_specs=[pl.BlockSpec(memory_space=pltpu.HBM)] * 6,
        out_specs=[pl.BlockSpec(memory_space=pltpu.VMEM)] * 2,
        scratch_shapes=[
            pltpu.VMEM((BASIS + 1, nx, ny, nz), f32),
            pltpu.VMEM((nx, ny, nz), f32),
            pltpu.VMEM((nx, ny, nz), f32),
            pltpu.VMEM((nx, ny, nz), f32),
            pltpu.VMEM((nx, ny, nz), f32),
            pltpu.VMEM((BASIS,) + block, f32),
            pltpu.VMEM((2 * nz, wide), jnp.bfloat16),
            pltpu.VMEM((nx, ny, wide), f32),
            pltpu.VMEM((16, LANES), f32),
            pltpu.VMEM((ITERS, sizes["gx"], sizes["gy"], sizes["gz"], BASIS, LANES), f32),
            pltpu.VMEM(block, jnp.int32),
            pltpu.VMEM((3,) + freqs[0].shape, jnp.int32),
            pltpu.SemaphoreType.DMA((6,)),
            pltpu.SemaphoreType.DMA((copies,)),
            pltpu.SemaphoreType.DMA((copies,)),
            pltpu.SemaphoreType.DMA((smalls,)),
            pltpu.SemaphoreType.DMA((smalls,)),
        ],
        compiler_params=pltpu.CompilerParams(
            collective_id=0, has_side_effects=True, vmem_limit_bytes=56 * 1024 * 1024
        ),
    )(right_side, diagonal, sign_bits, *freqs)


def solution(mesh):
    in_specs = (P("gx", "gy", "gz"), P("gx", "gy", "gz"), P("gx", "gy", "gz"), P(), P(), P())
    out_specs = (P("gx", "gy", "gz"), P("gx", "gy", "gz"))
    sizes = {axis: mesh.shape[axis] for axis in ("gx", "gy", "gz")}

    def run(right_side, diagonal, sign_bits, freq_x, freq_y, freq_z):
        plan = shards
        if whole_fits(sizes, *right_side.shape, freq_x.shape[0]):
            plan = functools.partial(whole_shards, sizes)
        mapped = jax.shard_map(
            plan, mesh=mesh, in_specs=in_specs, out_specs=out_specs, check_vma=False
        )
        return mapped(right_side, diagonal, sign_bits, freq_x, freq_y, freq_z)

    return run
```

```python
import functools
import math

import jax
import jax.numpy as jnp
from jax import lax
from jax.experimental import pallas as pl
from jax.experimental.pallas import tpu as pltpu
from jax.sharding import PartitionSpec as P

BASIS = 8
ITERS = 2


center_value = 7.0
half_range = 7.0
tiny_value = 1e-06
highest = lax.Precision.HIGHEST


def extended(shard, sides, width):
    for axis, dim in sides:
        size, length = (lax.axis_size(axis), shard.shape[dim])
        up = [(i, (i + 1) % size) for i in range(size - 1)]
        down = [(j, i) for i, j in up]
        last = lax.slice_in_dim(shard, length - width, length, axis=dim)
        first = lax.slice_in_dim(shard, 0, width, axis=dim)
        before = lax.ppermute(last, axis, up)
        after = lax.ppermute(first, axis, down)
        shard = jnp.concatenate([before, shard, after], axis=dim)
    return shard


def stencil(padded, diagonal):
    beside = padded[2:, 1:-1, 1:-1] + padded[:-2, 1:-1, 1:-1]
    beside = beside + padded[1:-1, 2:, 1:-1] + padded[1:-1, :-2, 1:-1]
    beside = beside + padded[1:-1, 1:-1, 2:] + padded[1:-1, 1:-1, :-2]
    return (6.0 + diagonal) * padded[1:-1, 1:-1, 1:-1] - beside


def cosine_table(freqs, offset, count, length):
    indices = offset + jnp.arange(count, dtype=jnp.int32)
    phases = (2 * indices[:, None] + 1) * freqs[None, :] % (4 * length)
    return (jnp.sqrt(2.0 / length) * jnp.cos(jnp.pi * phases / (2.0 * length))).astype(jnp.float32)


def least_squares(matrix):
    count = matrix.shape[0] - 1
    target = matrix[count]
    orthonormal = []
    upper = {}
    for column_at in range(count):
        column = matrix[column_at]
        for repeat in range(2):
            for earlier in range(column_at):
                amount = jnp.dot(orthonormal[earlier], column, precision=highest)
                column = column - amount * orthonormal[earlier]
                upper[earlier, column_at] = upper.get((earlier, column_at), 0.0) + amount
        length = jnp.sqrt(jnp.dot(column, column, precision=highest) + tiny_value)
        orthonormal.append(column / length)
        upper[column_at, column_at] = length
    projected = [jnp.dot(basis_row, target, precision=highest) for basis_row in orthonormal]
    solved = [None] * count
    for row_at in range(count - 1, -1, -1):
        value = projected[row_at]
        for later in range(row_at + 1, count):
            value = value - upper[row_at, later] * solved[later]
        solved[row_at] = value / upper[row_at, row_at]
    return jnp.stack(solved)


def basis_plain(residual, diagonal):
    vectors = [residual]
    images = []
    for position in range(BASIS):
        padded = extended(vectors[position], (("gx", 0), ("gy", 1), ("gz", 2)), 1)
        image = stencil(padded, diagonal)
        images.append(image)
        if position + 1 < BASIS:
            turned = (image - center_value * vectors[position]) / half_range
            vectors.append(turned if position == 0 else 2.0 * turned - vectors[position - 1])
    return (vectors, images)


def local_sketch(columns, signs, table_x, table_y, table_z):
    flipped = jnp.stack(columns, axis=2) * signs[:, :, None, :]
    size_x, size_y, count, depth = flipped.shape
    rows_flat = flipped.reshape(-1, depth)
    weights = table_x[:, None, :] * table_y[None, :, :]
    sampled = table_z.shape[1]
    block = min(512, sampled)
    pieces = []
    for begin in range(0, sampled, block):
        inner_sums = jnp.dot(
            rows_flat,
            table_z[:, begin : begin + block],
            precision=highest,
            preferred_element_type=jnp.float32,
        )
        inner_sums = inner_sums.reshape(size_x, size_y, count, block)
        pieces.append(
            jnp.einsum(
                "xyjs,xys->js", inner_sums, weights[:, :, begin : begin + block], precision=highest
            )
        )
    return jnp.concatenate(pieces, axis=1)


def shards(right_side, diagonal, sign_bits, freq_x, freq_y, freq_z):
    size_x, size_y, size_z = right_side.shape
    table_x = cosine_table(
        freq_x, lax.axis_index("gx") * size_x, size_x, size_x * lax.axis_size("gx")
    )
    table_y = cosine_table(
        freq_y, lax.axis_index("gy") * size_y, size_y, size_y * lax.axis_size("gy")
    )
    table_z = cosine_table(
        freq_z, lax.axis_index("gz") * size_z, size_z, size_z * lax.axis_size("gz")
    )
    signs = 1.0 - 2.0 * sign_bits.astype(jnp.float32)
    solution = jnp.zeros_like(right_side)
    residual = right_side
    for restart in range(ITERS):
        vectors, images = basis_plain(residual, diagonal)
        partial_value = local_sketch(images + [residual], signs, table_x, table_y, table_z)
        shares = lax.psum_scatter(partial_value, "gx", scatter_dimension=1, tiled=True)
        shares = lax.psum(shares, ("gy", "gz"))
        matrix = lax.all_gather(shares, "gx", axis=1, tiled=True)
        weights_solved = least_squares(matrix)
        for position in range(BASIS):
            solution = solution + weights_solved[position] * vectors[position]
            residual = residual - weights_solved[position] * images[position]
    return (solution, residual)


MESH = pl.DeviceIdType.MESH
LANES = 128
SINE = [(-1.0) ** k / math.factorial(2 * k + 1) for k in range(7)]


def cosines(freqs, count, length):
    cells = lax.broadcasted_iota(jnp.int32, (count, freqs.shape[1]), 0)
    phases = lax.rem((2 * cells + 1) * freqs, 4 * length)
    folded = length - jnp.minimum(phases, 4 * length - phases)
    angle = folded.astype(jnp.float32) * (math.pi / (2.0 * length))
    square = angle * angle
    value = jnp.full_like(angle, SINE[-1])
    for term in SINE[-2::-1]:
        value = value * square + term
    return value * angle * math.sqrt(2.0 / length)


def total_of(value):
    return jnp.sum(jnp.sum(value, axis=0, keepdims=True), axis=1, keepdims=True)


def swept(left, among, short):
    count, left, amounts = len(left), list(left), []
    for e in range(count):
        amount = left[e]
        amounts.append(amount)
        left[e] = amount * short[e]
        for f in range(count):
            if f != e:
                left[f] = left[f] - amount * among[max(e, f)][min(e, f)]
    return amounts, left


def solve_rows(rows, target):
    count = len(rows)
    inner = [[total_of(rows[i] * rows[j]) for j in range(i, count)] for i in range(count)]
    basis, onto, among, short, upper, inverse = [], [], [], [], {}, []
    for at_column in range(count):
        column, square, left = rows[at_column], inner[at_column][0], []
        amounts = [0.0] * at_column
        if at_column:
            first, _ = swept([onto[e][at_column] for e in range(at_column)], among, short)
            for e in range(at_column):
                column = column - first[e] * basis[e]
            start = [total_of(q * column) for q in basis]
            square = total_of(column * column)
            second, left = swept(start, among, short)
            for e in range(at_column):
                column = column - second[e] * basis[e]
                square = square - second[e] * (start[e] + left[e])
                amounts[e] = first[e] + second[e]
                upper[e, at_column] = amounts[e]
        scale = lax.rsqrt(jnp.maximum(square, 0.0) + tiny_value)
        basis.append(column * scale)
        along = {}
        for j in range(at_column + 1, count):
            value = inner[at_column][j - at_column]
            for e in range(at_column):
                value = value - amounts[e] * onto[e][j]
            along[j] = value * scale
        onto.append(along)
        among.append([value * scale for value in left])
        short.append(tiny_value * scale * scale)
        inverse.append(scale)
    projected = [total_of(q * target) for q in basis]
    solved = [None] * count
    for row in range(count - 1, -1, -1):
        value = projected[row]
        for later in range(row + 1, count):
            value = value - upper[row, later] * solved[later]
        solved[row] = value * inverse[row]
    return solved


class Gather:
    def __init__(self, sizes, block, send_sem, recv_sem):
        self.sizes, self.block = sizes, block
        self.send_sem, self.recv_sem = send_sem, recv_sem
        self.count = 0
        self.at = {axis: lax.axis_index(axis) for axis in sizes}

    def regions(self, ref, state, at):
        bx, by, bz = self.block
        gx, gy, gz = at["gx"], at["gy"], at["gz"]
        xs = slice(None) if state["x"] == "all" else pl.ds(gx * bx, bx)
        zs = slice(None) if state["z"] == "all" else pl.ds(pl.multiple_of(gz * bz, bz), bz)
        if state["y"] == "own":
            ys = [gy]
        else:
            ys = [lax.rem(gy, 2) + 2 * k for k in range(self.sizes["gy"] // 2)]
        return [ref.at[xs, pl.ds(pl.multiple_of(y * by, by), by), zs] for y in ys]

    def plan(self, ref, state, phase, held=None):
        axis = {"X": "gx", "Z": "gz", "H": "gy", "C": "gy"}[phase]
        size, here = self.sizes[axis], self.at[axis]
        if phase == "C":
            hops = [(here + 1 - 2 * lax.rem(here, 2), here + 1 - 2 * lax.rem(here, 2))]
        else:
            stride = 2 if phase == "H" else 1
            hops = [
                (lax.rem(here + k, size), lax.rem(here + size - k, size))
                for k in range(stride, size, stride)
            ]
        sends, arriving = [], []
        for target, origin in hops:
            mine = self.regions(ref, state, self.at)
            theirs = self.regions(ref, state, {**self.at, axis: origin})
            for source, landing in zip(mine, theirs):
                n = self.count
                self.count += 1
                sems = dict(send_sem=self.send_sem.at[n], recv_sem=self.recv_sem.at[n])
                go = dict(device_id={axis: target}, device_id_type=MESH)
                sends.append(
                    pltpu.make_async_remote_copy(
                        src_ref=source if held is None else held, dst_ref=source, **sems, **go
                    )
                )
                arriving.append(
                    pltpu.make_async_remote_copy(src_ref=landing, dst_ref=landing, **sems, **go)
                )
        if phase == "X":
            state["x"] = "all"
        elif phase == "Z":
            state["z"] = "all"
        elif phase == "H":
            state["y"] = "half"
        else:
            state["y"] = "all"
        return sends, arriving


def copies_needed(sizes):
    half = sizes["gy"] // 2
    return 3 * (sizes["gx"] - 1 + (sizes["gz"] - 1) * half + half - 1 + half) + 8


def whole_kernel(
    sizes, share, right_ref, diagonal_ref, bits_ref, fx_ref, fy_ref, fz_ref, sol_ref, res_ref,
    images, diag, sign, even, odd, kept, table, weights, rows, sums, bits, freqs, load_sem, send_sem,
    recv_sem, small_send, small_recv,
):
    bx, by, bz = right_ref.shape
    _, nx, ny, nz = images.shape
    wide = table.shape[1]
    cells = nx * ny
    at = {axis: lax.axis_index(axis) for axis in sizes}
    x0 = at["gx"] * bx
    y0 = pl.multiple_of(at["gy"] * by, by)
    z0 = pl.multiple_of(at["gz"] * bz, bz)
    own = (pl.ds(x0, bx), pl.ds(y0, by), pl.ds(z0, bz))
    field = images.at[BASIS]

    loads = [
        pltpu.make_async_copy(source, target, load_sem.at[n])
        for n, (source, target) in enumerate(
            [
                (right_ref, field.at[own]),
                (diagonal_ref, diag.at[own]),
                (bits_ref, bits),
                (fx_ref, freqs.at[0]),
                (fy_ref, freqs.at[1]),
                (fz_ref, freqs.at[2]),
            ]
        )
    ]
    for copy in loads:
        copy.start()
    barrier = pltpu.get_barrier_semaphore()
    side = sizes["gy"] * sizes["gz"]
    across = at["gy"] * sizes["gz"] + at["gz"]

    def member(index):
        return {"gy": lax.div(index, sizes["gz"]), "gz": lax.rem(index, sizes["gz"])}

    plane_hops = [
        (member(lax.rem(across + k, side)), member(lax.rem(across + side - k, side)))
        for k in range(1, side)
    ]
    line_hops = [
        (
            {"gx": lax.rem(at["gx"] + k, sizes["gx"])},
            {"gx": lax.rem(at["gx"] + sizes["gx"] - k, sizes["gx"])},
        )
        for k in range(1, sizes["gx"])
    ]
    for target, _ in plane_hops + line_hops:
        pl.semaphore_signal(barrier, inc=1, device_id=target, device_id_type=MESH)
    peers = len(plane_hops + line_hops)

    gather = Gather(sizes, (bx, by, bz), send_sem, recv_sem)
    plans = []
    for ref, order, held in [
        (field, "XZHC", right_ref),
        (diag, "XHZC", diagonal_ref),
        (sign, "XZHC", None),
    ]:
        state = {"x": "own", "y": "own", "z": "own"}
        plans.append(
            [gather.plan(ref, state, phase, held if phase == "X" else None) for phase in order]
        )

    def begin(array, step):
        for copy in plans[array][step][0]:
            copy.start()

    def arrive(array, step):
        for copy in plans[array][step][1]:
            copy.wait_recv()

    pl.semaphore_wait(barrier, peers)
    begin(0, 0)
    begin(1, 0)
    for copy in loads:
        copy.wait()
    sol_ref[...] = jnp.zeros_like(sol_ref)
    sign[own] = 1.0 - 2.0 * bits[...].astype(jnp.float32)
    begin(2, 0)

    me = (at["gx"] * sizes["gy"] + at["gy"]) * sizes["gz"] + at["gz"]
    lane = lax.broadcasted_iota(jnp.int32, (1, LANES), 1)

    def own_rows(number):
        begin_at = me * share
        row = freqs[number, pl.ds(begin_at // LANES, 1), :]
        part = lax.rem(begin_at, LANES) // share
        spread = row
        for k in range(LANES // share):
            turned = row
            for group in range(LANES // share):
                shift = ((group - k) * share) % LANES
                moved = pltpu.roll(row, shift, 1) if shift else row
                turned = jnp.where(lane // share == group, moved, turned)
            spread = jnp.where(part == k, turned, spread)
        return jnp.concatenate([spread] * (wide // LANES), axis=1)

    def tables():
        cos_x = cosines(own_rows(0), nx, nx)
        cos_y = cosines(own_rows(1), ny, ny)
        for x in range(nx):
            weights[x] = cos_x[x : x + 1] * cos_y
        group = lax.broadcasted_iota(jnp.int32, (nz, wide), 1) // share
        cos_z = cosines(own_rows(2), nz, nz)
        first = cos_z.astype(jnp.bfloat16).astype(jnp.float32)
        second = (cos_z - first).astype(jnp.bfloat16).astype(jnp.float32)
        third = cos_z - first - second
        chosen = jnp.where(group == 0, first, jnp.where(group == 1, second, third))
        held = jnp.where(group < 3, chosen, 0.0).astype(jnp.bfloat16)
        table[0:nz] = held
        table[nz : 2 * nz] = held

    for step in range(1, 4):
        for array in range(2):
            arrive(array, step - 1)
            begin(array, step)
        if step == 1:
            tables()
    arrive(0, 3)
    arrive(1, 3)

    def beside_along_y(plane):
        tiles = plane.reshape(ny // 8, 8, nz)
        row_at = lax.broadcasted_iota(jnp.int32, tiles.shape, 1)
        outside = jnp.zeros((1, 8, nz), jnp.float32)
        down, up = pltpu.roll(tiles, 1, 1), pltpu.roll(tiles, 7, 1)
        below = jnp.where(row_at == 0, jnp.concatenate([outside, down[:-1]], axis=0), down)
        above = jnp.where(row_at == 7, jnp.concatenate([up[1:], outside], axis=0), up)
        return (below + above).reshape(ny, nz)

    def beside_along_z(plane):
        parts = nz // LANES
        lane_at = lax.broadcasted_iota(jnp.int32, (ny, LANES), 1)
        cut = [plane[:, c * LANES : (c + 1) * LANES] for c in range(parts)]
        later = [pltpu.roll(part, 1, 1) for part in cut]
        sooner = [pltpu.roll(part, LANES - 1, 1) for part in cut]
        summed = []
        for c in range(parts):
            low = later[c - 1] if c else 0.0
            high = sooner[c + 1] if c + 1 < parts else 0.0
            summed.append(
                jnp.where(lane_at == 0, low, later[c])
                + jnp.where(lane_at == LANES - 1, high, sooner[c])
            )
        return jnp.concatenate(summed, axis=1)

    def stencil_step(j, here_ref, other_ref):
        factor = jnp.where(j == 0, 1.0 / half_range, 2.0 / half_range).astype(jnp.float32)
        kept[j] = here_ref[own]
        for x in range(nx):
            here = here_ref[x]
            beside = None
            for near in (x + 1, x - 1):
                if 0 <= near < nx:
                    beside = here_ref[near] if beside is None else beside + here_ref[near]
            beside = beside + beside_along_y(here) + beside_along_z(here)
            image = (6.0 + diag[x]) * here - beside
            images[j, x] = image
            other_ref[x] = (image - center_value * here) * factor - other_ref[x]

    def sketch_row(j):
        turned = (images[j] * sign[...]).reshape(cells, nz)
        high = turned.astype(jnp.bfloat16)
        low = (turned - high.astype(jnp.float32)).astype(jnp.bfloat16)
        both = jnp.concatenate([high, low], axis=1)
        sampled = jnp.dot(both, table[...], preferred_element_type=jnp.float32)
        sampled = sampled * weights[...].reshape(cells, wide)
        total = jnp.sum(sampled, axis=0, keepdims=True)
        folded = total[:, :LANES]
        for k in range(1, wide // LANES):
            folded = folded + total[:, k * LANES : (k + 1) * LANES]
        spread = folded
        for k in range(1, LANES // share):
            spread = spread + pltpu.roll(folded, k * share, 1)
        rows[pl.ds(j, 1), :] = spread

    @pl.loop(0, ITERS)
    def _(restart):
        for x in range(nx):
            even[x] = field[x]
            odd[x] = jnp.zeros((ny, nz), jnp.float32)

        @pl.loop(0, BASIS // 2)
        def _(pair):
            stencil_step(2 * pair, even, odd)
            stencil_step(2 * pair + 1, odd, even)
            for step in range(3):

                @pl.when((restart == 0) & (pair == step))
                def _():
                    arrive(2, step)
                    begin(2, step + 1)

        @pl.when(restart == 0)
        def _():
            arrive(2, 3)

        @pl.loop(0, BASIS + 1, unroll=BASIS + 1)
        def _(j):
            sketch_row(j)

        buffer = sums.at[restart]
        behind = (lane // share == 1) & (lax.broadcasted_iota(jnp.int32, (BASIS, LANES), 0) == 0)
        tile = jnp.where(behind, rows[BASIS : BASIS + 1, :], rows[0:BASIS, :])
        buffer[pl.ds(at["gx"], 1), pl.ds(at["gy"], 1), pl.ds(at["gz"], 1)] = tile.reshape(
            1, 1, 1, BASIS, LANES
        )

        def shares(place, whole):
            rest = [slice(None)] * 2 if whole else [pl.ds(place[axis], 1) for axis in ("gy", "gz")]
            return buffer.at[(pl.ds(place["gx"], 1), *rest)]

        small = restart * peers
        started = []
        for hops, whole in ((plane_hops, False), (line_hops, True)):
            arrivals = []
            for target, origin in hops:
                sems = dict(send_sem=small_send.at[small], recv_sem=small_recv.at[small])
                go = dict(device_id=target, device_id_type=MESH)
                small = small + 1
                source, landing = shares(at, whole), shares({**at, **origin}, whole)
                copy = pltpu.make_async_remote_copy(src_ref=source, dst_ref=source, **sems, **go)
                copy.start()
                started.append(copy)
                arrivals.append(
                    pltpu.make_async_remote_copy(src_ref=landing, dst_ref=landing, **sems, **go)
                )
            for copy in arrivals:
                copy.wait_recv()
        devices = math.prod(sizes.values())
        tiles = buffer[...].reshape(devices, BASIS, LANES)
        sketched = [jnp.where(lane < share, tiles[:, j, :], 0.0) for j in range(BASIS)]
        aside = pltpu.roll(tiles[:, 0, :], LANES - share, 1)
        solved = solve_rows(sketched, jnp.where(lane < share, aside, 0.0))
        for copy in started:
            copy.wait_send()

        total = sol_ref[...]
        for j in range(BASIS):
            total = total + solved[j].reshape(1, 1, 1) * kept[j]
        sol_ref[...] = total

        @pl.when(restart == 0)
        def _():
            for plan in plans:
                for sends, _ in plan:
                    for copy in sends:
                        copy.wait_send()

        @pl.when(restart == ITERS - 1)
        def _():
            left = field[own]
            for j in range(BASIS):
                left = left - solved[j].reshape(1, 1, 1) * images[(j,) + own]
            res_ref[...] = left

        @pl.when(restart < ITERS - 1)
        def _():
            for x in range(nx):
                left = field[x]
                for j in range(BASIS):
                    left = left - solved[j] * images[j, x]
                field[x] = left


def whole_fits(sizes, nx, ny, nz, sampled):
    devices = math.prod(sizes.values())
    share = sampled // devices
    if sizes["gy"] % 2 or sampled % devices or share == 0 or LANES % share or 2 * share > LANES:
        return False
    if nz % LANES or nz // sizes["gz"] != LANES or (ny // sizes["gy"]) % 8 or ny % 16:
        return False
    return nx * ny * nz * 4 * (2 * BASIS + 8) <= 24 * 1024 * 1024


def whole_shards(sizes, right_side, diagonal, sign_bits, freq_x, freq_y, freq_z):
    block = right_side.shape
    nx, ny, nz = (size * sizes[axis] for size, axis in zip(block, ("gx", "gy", "gz")))
    share = freq_x.shape[0] // math.prod(sizes.values())
    wide = -(-3 * share // LANES) * LANES
    freqs = [f.reshape(-1, LANES) for f in (freq_x, freq_y, freq_z)]
    f32 = jnp.float32
    copies = copies_needed(sizes)
    smalls = ITERS * (sizes["gx"] - 1 + sizes["gy"] * sizes["gz"] - 1)
    return pl.pallas_call(
        functools.partial(whole_kernel, sizes, share),
        out_shape=[jax.ShapeDtypeStruct(block, f32)] * 2,
        in_specs=[pl.BlockSpec(memory_space=pltpu.HBM)] * 6,
        out_specs=[pl.BlockSpec(memory_space=pltpu.VMEM)] * 2,
        scratch_shapes=[
            pltpu.VMEM((BASIS + 1, nx, ny, nz), f32),
            pltpu.VMEM((nx, ny, nz), f32),
            pltpu.VMEM((nx, ny, nz), f32),
            pltpu.VMEM((nx, ny, nz), f32),
            pltpu.VMEM((nx, ny, nz), f32),
            pltpu.VMEM((BASIS,) + block, f32),
            pltpu.VMEM((2 * nz, wide), jnp.bfloat16),
            pltpu.VMEM((nx, ny, wide), f32),
            pltpu.VMEM((16, LANES), f32),
            pltpu.VMEM((ITERS, sizes["gx"], sizes["gy"], sizes["gz"], BASIS, LANES), f32),
            pltpu.VMEM(block, jnp.int32),
            pltpu.VMEM((3,) + freqs[0].shape, jnp.int32),
            pltpu.SemaphoreType.DMA((6,)),
            pltpu.SemaphoreType.DMA((copies,)),
            pltpu.SemaphoreType.DMA((copies,)),
            pltpu.SemaphoreType.DMA((smalls,)),
            pltpu.SemaphoreType.DMA((smalls,)),
        ],
        compiler_params=pltpu.CompilerParams(
            collective_id=0, has_side_effects=True, vmem_limit_bytes=56 * 1024 * 1024
        ),
    )(right_side, diagonal, sign_bits, *freqs)


def solution(mesh):
    in_specs = (P("gx", "gy", "gz"), P("gx", "gy", "gz"), P("gx", "gy", "gz"), P(), P(), P())
    out_specs = (P("gx", "gy", "gz"), P("gx", "gy", "gz"))
    sizes = {axis: mesh.shape[axis] for axis in ("gx", "gy", "gz")}

    def run(right_side, diagonal, sign_bits, freq_x, freq_y, freq_z):
        plan = shards
        if whole_fits(sizes, *right_side.shape, freq_x.shape[0]):
            plan = functools.partial(whole_shards, sizes)
        mapped = jax.shard_map(
            plan, mesh=mesh, in_specs=in_specs, out_specs=out_specs, check_vma=False
        )
        return mapped(right_side, diagonal, sign_bits, freq_x, freq_y, freq_z)

    return run
```
